128 devices in a mesh: dp: 16 (over z, x), mp: 8 (over y, core).
Axes of the slice: x: 4, y: 4, z: 4, core: 2. Of those that a mesh axis runs over, the one named last changes fastest.
Arguments:
- queries: bfloat16 [8192, 8192], P('dp', 'mp'), may hold values from -160 to 160
- out_grad: bfloat16 [8192, 8192], P('dp', 'mp'), may hold values from -6 to 6
- response_keys: bfloat16 [8192, 1024], P('dp', 'mp'), may hold values from -6 to 6
- response_values: bfloat16 [8192, 1024], P('dp', 'mp'), may hold values from -6 to 6
- prefix_keys: bfloat16 [16384, 1024], P('dp', 'mp'), may hold values from -48 to 48
- prefix_values: bfloat16 [16384, 1024], P('dp', 'mp'), may hold values from -6 to 6
- q_weight: bfloat16 [8192, 8192], P(None, 'mp'), may hold values from -0.0625 to 0.0625
- block_prompt: int32 [32], P('dp'), may hold values from 0 to 15, as said below
- response_lengths: int32 [32, 4], P('dp'), may hold values from 1 to 128, 256 in all within a row
Outputs:
- input_grad: bfloat16 [8192, 8192], P('dp', 'mp')
- response_key_grad: bfloat16 [8192, 1024], P('dp', 'mp')
- response_value_grad: bfloat16 [8192, 1024], P('dp', 'mp')
- prefix_key_grad: bfloat16 [16384, 1024], P('dp', 'mp')
- prefix_value_grad: bfloat16 [16384, 1024], P('dp', 'mp')
The draws below stay inside these ranges and needn't reach their ends.
Inputs may be any that keep to these rules, and one draw needn't show every extreme that they name: `block_prompt`: every prompt is answered by at least one block; some prompts by several.
All inputs are finite; a program needn't handle non-finite values.
Results may differ from the reference program's by a relative error of at most 0.017.
Values may be sent and summed in bfloat16 or wider, within the bound.
A program may use at most 192 MiB of HBM per device.

```python
import math
import jax
import jax.numpy as jnp
import numpy as np
from jax import lax

D = 8192
HEADS = 64
KV_HEADS = 8
HEAD_DIM = 128
PREFIX = 1024
BLOCK = 256
SEGS = 4
BLOCKS = 32
PROMPTS = 16
ROWS = 8192
N_MP = 8


def draw_queries(key, part):
    key = jax.random.fold_in(key, 11)
    first = jax.random.fold_in(key, 0)
    base = jax.random.normal(first, (ROWS, HEADS * HEAD_DIM), jnp.float32)
    return jnp.clip(base, -160.0, 160.0).astype(jnp.bfloat16)


def draw_prefix_keys(key, part):
    key = jax.random.fold_in(key, 23)
    first = jax.random.fold_in(key, 0)
    count = PROMPTS * PREFIX
    base = jax.random.normal(first, (count, KV_HEADS * HEAD_DIM), jnp.float32)
    return jnp.clip(base, -48.0, 48.0).astype(jnp.bfloat16)


def draw_block_prompt(key, part):
    key = jax.random.fold_in(key, 3)
    keys = jax.random.split(key, 5)
    first = jax.random.permutation(keys[0], PROMPTS)
    extra = BLOCKS - PROMPTS
    lower = jnp.minimum(jax.random.randint(keys[1], (extra,), 0, PROMPTS), jax.random.randint(keys[2], (extra,), 0, PROMPTS))
    relabel = jax.random.permutation(keys[3], PROMPTS)
    rest = relabel[lower]
    return jax.random.permutation(keys[4], jnp.concatenate([first, rest])).astype(jnp.int32)


def block_scale(key, shape, cuts, least, high):
    gain = 1.0
    for position, parts in cuts:
        draws = jax.random.uniform(jax.random.fold_in(jax.random.fold_in(key, 6), position), (parts,), jnp.float32, least / len(cuts), high / len(cuts))
        gain = gain * jnp.repeat(jnp.exp(draws), shape[position] // parts).reshape((-1,) + (1,) * (len(shape) - 1 - position))
    return gain


def profile(number_of, total, most, skew):
    loads = [(1 << 20) // math.isqrt(grade ** skew) + 1 for grade in range(2, number_of + 1)]
    surplus, holding = total - most - (number_of - 1), [1] * (number_of - 1)
    while surplus > 0:
        candidates = [i for i in range(number_of - 1) if holding[i] < most]
        whole, left = sum([loads[i] for i in candidates]), surplus
        for i in candidates:
            more = min(most - holding[i], max(1, left * loads[i] // whole), surplus)
            holding[i] = holding[i] + more
            surplus = surplus - more
    return np.array([most] + holding)


def ragged(own_key, number_of, total, reach, lean):
    if number_of == 2:
        one = jax.random.randint(own_key, (), max(1, total - reach), min(reach, total - 1) + 1)
        return jnp.stack([one, total - one])
    sizes = jnp.asarray(profile(number_of, total, reach, lean), jnp.int32)
    twos = (number_of - 1) // 2
    giver, taker = sizes[1:1 + 2 * twos:2], sizes[2:2 + 2 * twos:2]
    slack = jnp.minimum(giver - 1, reach - taker)
    shifted = jax.random.randint(jax.random.fold_in(own_key, 1), (twos,), 0, 1 << 20) % (slack + 1)
    sizes = sizes.at[1:1 + 2 * twos:2].set(giver - shifted).at[2:2 + 2 * twos:2].set(taker + shifted)
    return sizes[jax.random.permutation(jax.random.fold_in(own_key, 2), number_of)]


def scatter_about(key, extent, scale, limit, cuts=(), held_as=jnp.bfloat16):
    entries = scale * jax.random.normal(key, extent, jnp.float32)
    if cuts:
        entries = entries * block_scale(key, extent, cuts, -0.22, 0.18)
    return jnp.clip(entries, -limit, limit).astype(held_as)


def setup_inputs(seed: int = 0) -> dict:
    key_of = jax.random.split(jax.random.key(seed), 10)
    queries = draw_queries(jax.random.fold_in(key_of[9], 71), 0)
    out_grad = scatter_about(key_of[1], (ROWS, HEADS * HEAD_DIM), 1.0, 6.0, ((0, 16), (1, 8)))
    response_keys = scatter_about(key_of[2], (ROWS, KV_HEADS * HEAD_DIM), 1.0, 6.0, ((0, 16), (1, 8)))
    response_values = scatter_about(key_of[3], (ROWS, KV_HEADS * HEAD_DIM), 1.0, 6.0, ((0, 16), (1, 8)))
    prefix_keys = draw_prefix_keys(jax.random.fold_in(key_of[9], 71), 0)
    prefix_values = scatter_about(key_of[5], (PROMPTS * PREFIX, KV_HEADS * HEAD_DIM), 1.0, 6.0, ((0, 16), (1, 8)))
    q_weight = scatter_about(key_of[6], (D, HEADS * HEAD_DIM), (HEADS * HEAD_DIM) ** -0.5, 0.0625, ((1, 8),))
    block_prompt = draw_block_prompt(jax.random.fold_in(key_of[9], 71), 0)
    response_lengths = jax.vmap(lambda own: ragged(own, SEGS, BLOCK, BLOCK // 2, 2))(jax.random.split(key_of[8], BLOCKS)).reshape((BLOCKS, SEGS)).astype(jnp.int32)
    return {"queries": queries, "out_grad": out_grad, "response_keys": response_keys, "response_values": response_values, "prefix_keys": prefix_keys, "prefix_values": prefix_values, "q_weight": q_weight, "block_prompt": block_prompt, "response_lengths": response_lengths}


def segment_rows(lengths, block):
    ends = jnp.cumsum(lengths.astype(jnp.int32), axis=-1).astype(jnp.int32)
    places = jnp.arange(block, dtype=jnp.int32)
    return jnp.sum((places[:, None] >= ends[None, :]).astype(jnp.int32), axis=1)


def block_grads(query, pre_k, pre_v, own_k, own_v, d_out, seg):
    f32 = jnp.float32
    high = lax.Precision.HIGHEST
    rows = query.shape[0]
    kvn = own_k.shape[1] // HEAD_DIM
    group = query.shape[1] // HEAD_DIM // kvn
    scale = HEAD_DIM ** -0.5
    quer = query.astype(f32).reshape(rows, kvn, group, HEAD_DIM)
    dout = d_out.astype(f32).reshape(rows, kvn, group, HEAD_DIM)
    keys = jnp.concatenate([pre_k, own_k], 0).astype(f32).reshape(-1, kvn, HEAD_DIM)
    vals = jnp.concatenate([pre_v, own_v], 0).astype(f32).reshape(-1, kvn, HEAD_DIM)
    score = jnp.einsum("rkgd,skd->kgrs", quer, keys, precision=high) * scale
    places = jnp.arange(rows, dtype=jnp.int32)
    own = (seg[None, :] == seg[:, None]) & (places[None, :] <= places[:, None])
    mask = jnp.concatenate([jnp.ones((rows, pre_k.shape[0]), bool), own], 1)
    score = jnp.where(mask, score, -1e30)
    top = jnp.max(score, axis=-1, keepdims=True)
    expo = jnp.exp(score - top)
    prob = expo / jnp.sum(expo, axis=-1, keepdims=True)
    prob_low = lax.optimization_barrier(prob.astype(jnp.bfloat16)).astype(f32)
    output = jnp.einsum("kgrs,skd->rkgd", prob_low, vals, precision=high)
    delta = jnp.sum(dout * output, axis=-1)
    dprob = jnp.einsum("rkgd,skd->kgrs", dout, vals, precision=high)
    dscore = prob * (dprob - jnp.transpose(delta, (1, 2, 0))[..., None])
    dscore_low = lax.optimization_barrier(dscore.astype(jnp.bfloat16)).astype(f32)
    query_grad = (jnp.einsum("kgrs,skd->rkgd", dscore_low, keys, precision=high) * scale).reshape(rows, -1).astype(jnp.bfloat16)
    key_grad = (jnp.einsum("kgrs,rkgd->skd", dscore_low, quer, precision=high) * scale).reshape(-1, kvn * HEAD_DIM)
    value_grad = jnp.einsum("kgrs,rkgd->skd", prob_low, dout, precision=high).reshape(-1, kvn * HEAD_DIM)
    prefix = pre_k.shape[0]
    return query_grad, key_grad[:prefix], value_grad[:prefix], key_grad[prefix:], value_grad[prefix:]


def reference(queries, out_grad, response_keys, response_values, prefix_keys, prefix_values, q_weight, block_prompt, response_lengths):
    width = KV_HEADS * HEAD_DIM

    def one_block(carry, index):
        table_k, table_v = carry
        start = (block_prompt[index] * PREFIX).astype(jnp.int32)
        first = (index * BLOCK).astype(jnp.int32)
        pre_k = lax.dynamic_slice_in_dim(prefix_keys, start, PREFIX, 0)
        pre_v = lax.dynamic_slice_in_dim(prefix_values, start, PREFIX, 0)
        query = lax.dynamic_slice_in_dim(queries, first, BLOCK, 0)
        d_out = lax.dynamic_slice_in_dim(out_grad, first, BLOCK, 0)
        own_k = lax.dynamic_slice_in_dim(response_keys, first, BLOCK, 0)
        own_v = lax.dynamic_slice_in_dim(response_values, first, BLOCK, 0)
        seg = segment_rows(response_lengths[index], BLOCK)
        query_grad, pre_dk, pre_dv, own_dk, own_dv = block_grads(query, pre_k, pre_v, own_k, own_v, d_out, seg)
        table_k = lax.dynamic_update_slice_in_dim(table_k, lax.dynamic_slice_in_dim(table_k, start, PREFIX, 0) + pre_dk, start, 0)
        table_v = lax.dynamic_update_slice_in_dim(table_v, lax.dynamic_slice_in_dim(table_v, start, PREFIX, 0) + pre_dv, start, 0)
        return (table_k, table_v), (query_grad, own_dk.astype(jnp.bfloat16), own_dv.astype(jnp.bfloat16))

    empty = jnp.zeros((PROMPTS * PREFIX, width), jnp.float32)
    tables, grads = lax.scan(one_block, (empty, empty), jnp.arange(BLOCKS, dtype=jnp.int32))
    table_k, table_v = tables
    query_grad, own_dk, own_dv = grads
    query_grad = query_grad.reshape(ROWS, HEADS * HEAD_DIM)
    part_width = HEADS * HEAD_DIM // N_MP
    total = jnp.zeros((ROWS, D), jnp.float32)
    for shard in range(N_MP):
        lower = shard * part_width
        upper = lower + part_width
        partial_value = lax.dot_general(query_grad[:, lower:upper], q_weight[:, lower:upper], (((1,), (1,)), ((), ())), preferred_element_type=jnp.float32)
        total = total + lax.optimization_barrier(partial_value.astype(jnp.bfloat16)).astype(jnp.float32)
    return (total.astype(jnp.bfloat16), own_dk.reshape(ROWS, width), own_dv.reshape(ROWS, width), table_k.astype(jnp.bfloat16), table_v.astype(jnp.bfloat16))
```

```python
import functools

import jax
import jax.numpy as jnp
from jax import lax
from jax.experimental import pallas as pl
from jax.experimental.pallas import tpu as pltpu
from jax.sharding import PartitionSpec as P

HEAD_DIM = 128
GROUP = 16
SCALE = HEAD_DIM ** (-0.5)
LOG2E = 1.4426950408889634
MESH = pl.DeviceIdType.MESH
F32 = jnp.float32
BF16 = jnp.bfloat16


def dot(a, b):
    return jnp.dot(a, b, preferred_element_type=F32)


def dot_nt(a, b):
    return lax.dot_general(a, b, (((1,), (1,)), ((), ())), preferred_element_type=F32)


def fold(x, op):
    rows, cols = x.shape
    return op(x.reshape(rows // 8, 8, cols), axis=0)


def kernel(
    n,
    nmp,
    prompt_ref,
    lengths_ref,
    q_hbm,
    do_hbm,
    rk_hbm,
    rv_hbm,
    pk_hbm,
    pv_hbm,
    w_hbm,
    out_hbm,
    own_hbm,
    pre_hbm,
    q_v,
    do_v,
    own_v,
    w_v,
    tile_v,
    table_v,
    spread_v,
    choose_v,
    send_v,
    pre_v,
    keys_t,
    score_v,
    dprob_v,
    grad_v,
    qg_v,
    ownout_v,
    back_v,
    gather_v,
    home_v,
    part_v,
    sib_v,
    opp_v,
    hop_v,
    near_v,
    side_v,
    sum_v,
    in_sem,
    w_sem,
    s1_send,
    s1_recv,
    t_send,
    t_recv,
    s2_send,
    s2_recv,
    b_send,
    b_recv,
    h_send,
    h_recv,
    sib_send,
    sib_recv,
    opp_send,
    opp_recv,
    raw_send,
    raw_recv,
    mix_send,
    mix_recv,
    out_sem,
):
    me = lax.axis_index("dp")
    mp = lax.axis_index("mp")
    ny = nmp // 2
    y, core = mp // 2, lax.rem(mp, 2)
    y_right, y_left, y_opp = lax.rem(y + 1, ny), lax.rem(y + ny - 1, ny), lax.rem(y + 2, ny)
    right, left, sibling = y_right * 2 + core, y_left * 2 + core, y * 2 + 1 - core
    blocks, block = q_v.shape[0], q_v.shape[1]
    chunk = spread_v.shape[1]
    width = sib_v.shape[2]
    half = width // 2
    heads = q_v.shape[2] // HEAD_DIM
    tiles = score_v.shape[0] - 1
    per_tile = n // tiles

    def load(j, what, src, dst):
        return pltpu.make_async_copy(src, dst, in_sem.at[j, what])

    def own_loads(j):
        rows = pl.ds(j * block, block)
        return [
            load(j, 0, q_hbm.at[rows], q_v.at[j]),
            load(j, 1, do_hbm.at[rows], do_v.at[j]),
            load(j, 2, rk_hbm.at[rows], own_v.at[j, :, pl.ds(0, HEAD_DIM)]),
            load(j, 3, rv_hbm.at[rows], own_v.at[j, :, pl.ds(HEAD_DIM, HEAD_DIM)]),
        ]

    def w_load(dest):
        rows = pl.ds(pl.multiple_of(dest * width, width), width)
        return pltpu.make_async_copy(w_hbm.at[rows], w_v.at[rows], w_sem.at[dest])

    for j in range(blocks):
        for copy in own_loads(j):
            copy.start()

    barrier = pltpu.get_barrier_semaphore()

    def greet(o, carry):
        pl.semaphore_signal(
            barrier, inc=1, device_id={"dp": lax.rem(me + o, n)}, device_id_type=MESH
        )
        return carry

    lax.fori_loop(1, n, greet, 0)
    for other in (right, left, sibling):
        pl.semaphore_signal(barrier, inc=1, device_id={"mp": other}, device_id_type=MESH)
    for j in range(blocks):
        tile_v[j] = jnp.full((GROUP, HEAD_DIM), prompt_ref[j], jnp.int32).astype(F32).astype(BF16)
    pl.semaphore_wait(barrier, n - 1 + 3)

    def spread(o, carry):
        peer = lax.rem(me + o, n)
        rows = pl.ds(pl.multiple_of(peer * chunk, chunk), chunk)
        pltpu.make_async_remote_copy(
            src_ref=tile_v,
            dst_ref=table_v.at[me],
            send_sem=t_send,
            recv_sem=t_recv,
            device_id={"dp": peer},
            device_id_type=MESH,
        ).start()
        for what, src in ((0, pk_hbm), (1, pv_hbm)):
            pltpu.make_async_remote_copy(
                src_ref=src.at[rows],
                dst_ref=spread_v.at[me, :, pl.ds(what * HEAD_DIM, HEAD_DIM)],
                send_sem=s1_send,
                recv_sem=s1_recv,
                device_id={"dp": peer},
                device_id_type=MESH,
            ).start()
        return carry

    lax.fori_loop(1, n, spread, 0)
    mine = pl.ds(pl.multiple_of(me * chunk, chunk), chunk)
    pltpu.make_async_copy(tile_v, table_v.at[me], t_recv).start()
    for what, src in ((0, pk_hbm), (1, pv_hbm)):
        pltpu.make_async_copy(
            src.at[mine], spread_v.at[me, :, pl.ds(what * HEAD_DIM, HEAD_DIM)], s1_recv
        ).start()
    for dest in range(nmp):
        w_load(dest).start()

    pltpu.make_async_copy(table_v, table_v, t_recv).wait()
    side = n * GROUP
    row = lax.broadcasted_iota(jnp.int32, (side, side), 0)
    col = lax.broadcasted_iota(jnp.int32, (side, side), 1)
    same = lax.rem(row, GROUP) == lax.rem(col, GROUP)
    prompt_of_col = (col // GROUP).astype(F32)
    for j in range(blocks):
        wanted = table_v[:, j].reshape(side, HEAD_DIM).astype(F32)
        if side > HEAD_DIM:
            wanted = jnp.concatenate([wanted] * (side // HEAD_DIM), axis=1)
        else:
            wanted = wanted[:, :side]
        choose_v[j] = jnp.where(same & (wanted == prompt_of_col), 1.0, 0.0).astype(BF16)

    pltpu.make_async_copy(spread_v, spread_v, s1_recv).wait()
    for j in range(blocks):
        for g in range(chunk // GROUP):
            rows = pl.ds(g * GROUP, GROUP)
            picked = dot(choose_v[j], spread_v[:, rows, :].reshape(side, 2 * HEAD_DIM))
            send_v[j, :, rows, :] = picked.astype(BF16).reshape(n, GROUP, 2 * HEAD_DIM)

        def deliver(o, carry):
            peer = lax.rem(me + o, n)
            pltpu.make_async_remote_copy(
                src_ref=send_v.at[j, peer],
                dst_ref=pre_v.at[j, me],
                send_sem=s2_send.at[j],
                recv_sem=s2_recv.at[j],
                device_id={"dp": peer},
                device_id_type=MESH,
            ).start()
            return carry

        lax.fori_loop(1, n, deliver, 0)
        pltpu.make_async_copy(send_v.at[j, me], pre_v.at[j, me], s2_recv.at[j]).start()

    key_cols, value_cols = pl.ds(0, HEAD_DIM), pl.ds(HEAD_DIM, HEAD_DIM)

    def part_of(j, t, cols):
        if t == tiles:
            return own_v[j, :, cols]
        got = pre_v[j, t * per_tile : (t + 1) * per_tile, :, cols]
        return got.reshape(block, HEAD_DIM)

    def visible(j):
        place = lax.broadcasted_iota(jnp.int32, (block, block), 1)
        key = lax.broadcasted_iota(jnp.int32, (block, block), 0)
        end = lengths_ref[j, 0]
        first = jnp.where(place >= end, end, 0)
        for s in range(1, lengths_ref.shape[1] - 1):
            end = end + lengths_ref[j, s]
            first = jnp.where(place >= end, end, first)
        return (key >= first) & (key <= place)

    def prepare(j):
        for copy in own_loads(j):
            copy.wait()
        pltpu.make_async_copy(pre_v.at[j], pre_v.at[j], s2_recv.at[j]).wait()
        for t in range(tiles + 1):
            keys_t[:, t * block : (t + 1) * block] = part_of(j, t, key_cols).T
        grad_v[...] = jnp.zeros_like(grad_v)

    def attend(j, lower, upper):
        def head(h, carry):
            cols = pl.ds(pl.multiple_of(h * HEAD_DIM, HEAD_DIM), HEAD_DIM)
            qh, doh = q_v[j, :, cols], do_v[j, :, cols]
            top = None
            for t in range(tiles + 1):
                s = dot_nt(part_of(j, t, key_cols), qh)
                if t == tiles:
                    s = jnp.where(visible(j), s, -1e30)
                score_v[t] = s
                got = fold(s, jnp.max)
                top = got if top is None else jnp.maximum(top, got)
            top = jnp.max(top, axis=0, keepdims=True)
            total = jnp.zeros((8, block), F32)
            mixed = jnp.zeros((8, block), F32)
            for t in range(tiles + 1):
                dp = dot_nt(part_of(j, t, value_cols), doh)
                dprob_v[t] = dp
                e = jnp.exp2((score_v[t] - top) * (SCALE * LOG2E))
                score_v[t] = e
                total += fold(e, jnp.sum)
                mixed += fold(e * dp, jnp.sum)
            inverse = 1.0 / jnp.sum(total, axis=0, keepdims=True)
            delta = jnp.sum(mixed, axis=0, keepdims=True) * inverse
            dq = jnp.zeros((HEAD_DIM, block), F32)
            for t in range(tiles + 1):
                prob = score_v[t] * inverse
                ds = (prob * (dprob_v[t] - delta)).astype(BF16)
                grad_v[t, :, key_cols] += dot(ds, qh)
                grad_v[t, :, value_cols] += dot(prob.astype(BF16), doh)
                dq += dot(keys_t[:, t * block : (t + 1) * block], ds)
            qg_v[j, cols, :] = (dq * SCALE).astype(BF16)
            return carry

        lax.fori_loop(lower, upper, head, 0)

    def rounded(t):
        return jnp.concatenate(
            [grad_v[t, :, key_cols] * SCALE, grad_v[t, :, value_cols]], axis=1
        ).astype(BF16)

    def give_back(j):
        for t in range(tiles):
            back_v[j, t * per_tile : (t + 1) * per_tile] = rounded(t).reshape(
                per_tile, chunk, 2 * HEAD_DIM
            )
        ownout_v[j] = rounded(tiles)
        pltpu.make_async_copy(
            ownout_v.at[j], own_hbm.at[pl.ds(j * block, block)], out_sem.at[j, 0]
        ).start()

        def deliver(o, carry):
            peer = lax.rem(me + o, n)
            pltpu.make_async_remote_copy(
                src_ref=back_v.at[j, peer],
                dst_ref=gather_v.at[j, me],
                send_sem=b_send.at[j],
                recv_sem=b_recv.at[j],
                device_id={"dp": peer},
                device_id_type=MESH,
            ).start()
            return carry

        lax.fori_loop(1, n, deliver, 0)
        pltpu.make_async_copy(back_v.at[j, me], gather_v.at[j, me], b_recv.at[j]).start()

    def bring_home():
        for j in range(blocks):
            pltpu.make_async_copy(gather_v.at[j], gather_v.at[j], b_recv.at[j]).wait()
        pick = [choose_v[j].astype(F32).T.astype(BF16) for j in range(blocks)]
        for g in range(chunk // GROUP):
            rows = pl.ds(g * GROUP, GROUP)
            added = jnp.zeros((side, 2 * HEAD_DIM), F32)
            for j in range(blocks):
                added += dot(pick[j], gather_v[j, :, rows, :].reshape(side, 2 * HEAD_DIM))
            home_v[:, rows, :] = added.astype(BF16).reshape(n, GROUP, 2 * HEAD_DIM)

        def deliver(o, carry):
            peer = lax.rem(me + o, n)
            pltpu.make_async_remote_copy(
                src_ref=home_v.at[peer],
                dst_ref=pre_hbm.at[me],
                send_sem=h_send,
                recv_sem=h_recv,
                device_id={"dp": peer},
                device_id_type=MESH,
            ).start()
            return carry

        lax.fori_loop(1, n, deliver, 0)
        pltpu.make_async_copy(home_v.at[me], pre_hbm.at[me], h_recv).start()

    def project(j, dest):
        if j == 0:
            w_load(dest).wait()
        step = min(512, width)

        def tile(i, carry):
            rows = pl.ds(pl.multiple_of(i * step, step), step)
            from_w = pl.ds(pl.multiple_of(dest * width + i * step, step), step)
            part_v[j, dest, rows, :] = dot(w_v[from_w, :], qg_v[j]).astype(BF16)
            return carry

        lax.fori_loop(0, width // step, tile, 0)

    def to_sibling(j, y_dest, slot):
        return pltpu.make_async_remote_copy(
            src_ref=part_v.at[j, y_dest * 2 + 1 - core],
            dst_ref=sib_v.at[j, slot],
            send_sem=sib_send.at[j, slot],
            recv_sem=sib_recv.at[j, slot],
            device_id={"mp": sibling},
            device_id_type=MESH,
        )

    def remote(src, dst, send, recv, dest):
        return pltpu.make_async_remote_copy(
            src_ref=src,
            dst_ref=dst,
            send_sem=send,
            recv_sem=recv,
            device_id={"mp": dest},
            device_id_type=MESH,
        )

    halves, ways = (pl.ds(0, half), pl.ds(half, half)), (right, left)

    def opposite(j, way):
        src = opp_v.at[j, halves[way]]
        return remote(src, hop_v.at[j, way], opp_send.at[j, way], opp_recv.at[j, way], ways[way])

    def raw(j, way):
        rows = halves[1 - way]
        src, dst = near_v.at[j, way, rows], side_v.at[j, way, rows]
        return remote(src, dst, raw_send.at[j, way], raw_recv.at[j, way], ways[way])

    def mixed(j, way):
        rows = halves[way]
        src, dst = near_v.at[j, way, rows], side_v.at[j, way, rows]
        return remote(src, dst, mix_send.at[j, way], mix_recv.at[j, way], ways[way])

    def chip_sum(j, y_dest, slot, rows):
        mine = part_v[j, y_dest * 2 + core, rows, :].astype(F32)
        return mine + sib_v[j, slot, rows, :].astype(F32)

    def send_partials(j):
        project(j, y_opp * 2 + 1 - core)
        to_sibling(j, y_opp, 0).start()
        project(j, y_opp * 2 + core)
        project(j, y_right * 2 + 1 - core)
        to_sibling(j, y_right, 1).start()
        to_sibling(j, y_opp, 0).wait_recv()
        opp_v[j] = chip_sum(j, y_opp, 0, slice(None)).astype(BF16)
        for way in range(2):
            opposite(j, way).start()
        project(j, y_left * 2 + 1 - core)
        to_sibling(j, y_left, 2).start()
        project(j, y_right * 2 + core)
        to_sibling(j, y_right, 1).wait_recv()
        near_v[j, 0] = chip_sum(j, y_right, 1, slice(None)).astype(BF16)
        raw(j, 0).start()
        project(j, y_left * 2 + core)
        to_sibling(j, y_left, 2).wait_recv()
        near_v[j, 1] = chip_sum(j, y_left, 2, slice(None)).astype(BF16)
        raw(j, 1).start()
        project(j, y * 2 + 1 - core)
        to_sibling(j, y, 3).start()
        project(j, y * 2 + core)

    def pass_on(j):
        for way, rows in enumerate(halves):
            opposite(j, way).wait_recv()
            near_v[j, way, rows, :] = (
                near_v[j, way, rows, :].astype(F32) + hop_v[j, way].astype(F32)
            ).astype(BF16)
            mixed(j, way).start()

    def finish(j):
        to_sibling(j, y, 3).wait_recv()
        for way in range(2):
            raw(j, way).wait_recv()
            mixed(j, way).wait_recv()
        added = chip_sum(j, y, 3, slice(None))
        added += side_v[j, 0].astype(F32) + side_v[j, 1].astype(F32)
        sum_v[j] = added.astype(BF16)
        pltpu.make_async_copy(
            sum_v.at[j], out_hbm.at[:, pl.ds(j * block, block)], out_sem.at[j, 1]
        ).start()

    prepare(0)
    attend(0, 0, heads)
    give_back(0)
    send_partials(0)
    prepare(1)
    attend(1, 0, heads // 2)
    pass_on(0)
    attend(1, heads // 2, heads)
    give_back(1)
    send_partials(1)
    bring_home()
    pass_on(1)
    finish(0)
    finish(1)

    def all_but_one(ref, sem):
        part = ref.at[pl.ds(0, n - 1)]
        pltpu.make_async_copy(part, part, sem).wait()

    all_but_one(table_v, t_send)
    all_but_one(spread_v, s1_send)
    all_but_one(home_v, h_send)
    for j in range(blocks):
        all_but_one(send_v.at[j], s2_send.at[j])
        all_but_one(back_v.at[j], b_send.at[j])
        for slot, y_dest in enumerate((y_opp, y_right, y_left, y)):
            to_sibling(j, y_dest, slot).wait_send()
        for way in range(2):
            opposite(j, way).wait_send()
            raw(j, way).wait_send()
            mixed(j, way).wait_send()
        pltpu.make_async_copy(
            ownout_v.at[j], own_hbm.at[pl.ds(j * block, block)], out_sem.at[j, 0]
        ).wait()
        pltpu.make_async_copy(
            sum_v.at[j], out_hbm.at[:, pl.ds(j * block, block)], out_sem.at[j, 1]
        ).wait()
    pltpu.make_async_copy(pre_hbm, pre_hbm, h_recv).wait()


def shards(
    queries,
    out_grad,
    response_keys,
    response_values,
    prefix_keys,
    prefix_values,
    q_weight,
    block_prompt,
    response_lengths,
):
    n, nmp = lax.axis_size("dp"), lax.axis_size("mp")
    blocks = block_prompt.shape[0]
    rows, cols = queries.shape
    block = rows // blocks
    prefix = prefix_keys.shape[0]
    chunk = prefix // n
    tiles = prefix // block
    width = q_weight.shape[0] // nmp
    two = 2 * HEAD_DIM
    dma = pltpu.SemaphoreType.DMA
    any_space = pl.BlockSpec(memory_space=pl.ANY)
    smem = pl.BlockSpec(memory_space=pltpu.SMEM)
    flops = 2 * rows * cols * (5 * (prefix + block) + q_weight.shape[0])
    out, own, pre = pl.pallas_call(
        functools.partial(kernel, n, nmp),
        out_shape=(
            jax.ShapeDtypeStruct((width, rows), BF16),
            jax.ShapeDtypeStruct((rows, two), BF16),
            jax.ShapeDtypeStruct((n, chunk, two), BF16),
        ),
        in_specs=[smem, smem] + [any_space] * 7,
        out_specs=(any_space,) * 3,
        scratch_shapes=[
            pltpu.VMEM((blocks, block, cols), BF16),
            pltpu.VMEM((blocks, block, cols), BF16),
            pltpu.VMEM((blocks, block, two), BF16),
            pltpu.VMEM(q_weight.shape, BF16),
            pltpu.VMEM((blocks, GROUP, HEAD_DIM), BF16),
            pltpu.VMEM((n, blocks, GROUP, HEAD_DIM), BF16),
            pltpu.VMEM((n, chunk, two), BF16),
            pltpu.VMEM((blocks, n * GROUP, n * GROUP), BF16),
            pltpu.VMEM((blocks, n, chunk, two), BF16),
            pltpu.VMEM((blocks, n, chunk, two), BF16),
            pltpu.VMEM((HEAD_DIM, prefix + block), BF16),
            pltpu.VMEM((tiles + 1, block, block), F32),
            pltpu.VMEM((tiles + 1, block, block), F32),
            pltpu.VMEM((tiles + 1, block, two), F32),
            pltpu.VMEM((blocks, cols, block), BF16),
            pltpu.VMEM((blocks, block, two), BF16),
            pltpu.VMEM((blocks, n, chunk, two), BF16),
            pltpu.VMEM((blocks, n, chunk, two), BF16),
            pltpu.VMEM((n, chunk, two), BF16),
            pltpu.VMEM((blocks, nmp, width, block), BF16),
            pltpu.VMEM((blocks, nmp // 2, width, block), BF16),
            pltpu.VMEM((blocks, width, block), BF16),
            pltpu.VMEM((blocks, 2, width // 2, block), BF16),
            pltpu.VMEM((blocks, 2, width, block), BF16),
            pltpu.VMEM((blocks, 2, width, block), BF16),
            pltpu.VMEM((blocks, width, block), BF16),
            dma((blocks, 4)),
            dma((nmp,)),
            dma,
            dma,
            dma,
            dma,
            dma((blocks,)),
            dma((blocks,)),
            dma((blocks,)),
            dma((blocks,)),
            dma,
            dma,
            dma((blocks, 4)),
            dma((blocks, 4)),
            dma((blocks, 2)),
            dma((blocks, 2)),
            dma((blocks, 2)),
            dma((blocks, 2)),
            dma((blocks, 2)),
            dma((blocks, 2)),
            dma((blocks, 2)),
        ],
        compiler_params=pltpu.CompilerParams(
            collective_id=0, has_side_effects=True, vmem_limit_bytes=60 * 2**20
        ),
        cost_estimate=pl.CostEstimate(
            flops=flops, bytes_accessed=2 * q_weight.size, transcendentals=0
        ),
        name="attention_backward",
    )(
        block_prompt,
        response_lengths,
        queries,
        out_grad,
        response_keys,
        response_values,
        prefix_keys,
        prefix_values,
        q_weight,
    )
    pre = pre.reshape(prefix, two)
    return (
        out.T,
        own[:, :HEAD_DIM],
        own[:, HEAD_DIM:],
        pre[:, :HEAD_DIM],
        pre[:, HEAD_DIM:],
    )


def solution(mesh):
    return jax.shard_map(
        shards,
        mesh=mesh,
        in_specs=(
            P("dp", "mp"),
            P("dp", "mp"),
            P("dp", "mp"),
            P("dp", "mp"),
            P("dp", "mp"),
            P("dp", "mp"),
            P(None, "mp"),
            P("dp"),
            P("dp", None),
        ),
        out_specs=(P("dp", "mp"), P("dp", "mp"), P("dp", "mp"), P("dp", "mp"), P("dp", "mp")),
        check_vma=False,
    )
```

```python
import functools

import jax
import jax.numpy as jnp
from jax import lax
from jax.experimental import pallas as pl
from jax.experimental.pallas import tpu as pltpu
from jax.sharding import PartitionSpec as P

HEAD_DIM = 128
GROUP = 16
SCALE = HEAD_DIM ** (-0.5)
LOG2E = 1.4426950408889634
MESH = pl.DeviceIdType.MESH
F32 = jnp.float32
BF16 = jnp.bfloat16


def dot(a, b):
    return jnp.dot(a, b, preferred_element_type=F32)


def dot_nt(a, b):
    return lax.dot_general(a, b, (((1,), (1,)), ((), ())), preferred_element_type=F32)


def fold(x, op):
    rows, cols = x.shape
    return op(x.reshape(rows // 8, 8, cols), axis=0)


def kernel(
    n,
    nmp,
    prompt_ref,
    lengths_ref,
    q_hbm,
    do_hbm,
    rk_hbm,
    rv_hbm,
    pk_hbm,
    pv_hbm,
    w_hbm,
    out_hbm,
    own_hbm,
    pre_hbm,
    q_v,
    do_v,
    own_v,
    w_v,
    table_v,
    stage_v,
    spread_v,
    choose_v,
    send_v,
    pre_v,
    keys_t,
    score_v,
    dprob_v,
    mask_v,
    grad_v,
    qg_v,
    ownout_v,
    back_v,
    gather_v,
    home_v,
    part_v,
    sib_v,
    hop_v,
    side_v,
    sum_v,
    in_sem,
    w_sem,
    t_send,
    t_recv,
    s1_sem,
    s1_send,
    s1_recv,
    s2_send,
    s2_recv,
    b_send,
    b_recv,
    h_send,
    h_recv,
    sib_send,
    sib_recv,
    opp_send,
    opp_recv,
    raw_send,
    raw_recv,
    mix_send,
    mix_recv,
    out_sem,
):
    me = lax.axis_index("dp")
    mp = lax.axis_index("mp")
    ny = nmp // 2
    y, core = mp // 2, lax.rem(mp, 2)
    y_right, y_left, y_opp = lax.rem(y + 1, ny), lax.rem(y + ny - 1, ny), lax.rem(y + 2, ny)
    right, left, sibling = y_right * 2 + core, y_left * 2 + core, y * 2 + 1 - core
    blocks, block = q_v.shape[0], q_v.shape[1]
    chunk = send_v.shape[2]
    width = sib_v.shape[2]
    half = width // 2
    heads = q_v.shape[2] // HEAD_DIM
    tiles = score_v.shape[1] - 1
    per_tile = n // tiles

    def load(j, what, src, dst):
        return pltpu.make_async_copy(src, dst, in_sem.at[j, what])

    def own_loads(j):
        rows = pl.ds(j * block, block)
        return [
            load(j, 0, q_hbm.at[rows], q_v.at[j]),
            load(j, 1, do_hbm.at[rows], do_v.at[j]),
            load(j, 2, rk_hbm.at[rows], own_v.at[j, :, pl.ds(0, HEAD_DIM)]),
            load(j, 3, rv_hbm.at[rows], own_v.at[j, :, pl.ds(HEAD_DIM, HEAD_DIM)]),
        ]

    def w_load(dest):
        rows = pl.ds(pl.multiple_of(dest * width, width), width)
        return pltpu.make_async_copy(w_hbm.at[rows], w_v.at[rows], w_sem.at[dest])

    key_cols, value_cols = pl.ds(0, HEAD_DIM), pl.ds(HEAD_DIM, HEAD_DIM)
    side = n * GROUP

    def prompt_loads():
        return [
            pltpu.make_async_copy(src, stage_v.at[:, :, cols], s1_sem.at[what])
            for what, src, cols in ((0, pk_hbm, key_cols), (1, pv_hbm, value_cols))
        ]

    for copy in prompt_loads():
        copy.start()
    for j in range(blocks):
        for copy in own_loads(j):
            copy.start()

    side_x = 4 if n == 16 else n
    if n == 16:
        ones = [(0, 1), (0, 3), (1, 0), (3, 0), (1, 1), (3, 3), (1, 3), (3, 1)]
        offsets = ones + [(0, 2), (2, 0), (1, 2), (3, 2), (2, 1), (2, 3), (2, 2)]
    else:
        offsets = [(0, o) for o in range(1, n)]
    side_z = n // side_x
    my_z, my_x = me // side_x, lax.rem(me, side_x)
    peers = [
        lax.rem(my_z + dz, side_z) * side_x + lax.rem(my_x + dx, side_x) for dz, dx in offsets
    ]

    barrier = pltpu.get_barrier_semaphore()
    for peer in peers:
        pl.semaphore_signal(barrier, inc=1, device_id={"dp": peer}, device_id_type=MESH)
    for other in (right, left, sibling):
        pl.semaphore_signal(barrier, inc=1, device_id={"mp": other}, device_id_type=MESH)
    for j in range(blocks):
        table_v[me, j, :] = jnp.full((HEAD_DIM,), prompt_ref[j], jnp.int32)
    for copy in prompt_loads():
        copy.wait()
    pl.semaphore_wait(barrier, n - 1 + 3)

    def to_all(src, dst, send, recv):
        for peer in peers:
            pltpu.make_async_remote_copy(
                src_ref=src.at[peer],
                dst_ref=dst.at[me],
                send_sem=send,
                recv_sem=recv,
                device_id={"dp": peer},
                device_id_type=MESH,
            ).start()
        pltpu.make_async_copy(src.at[me], dst.at[me], recv).start()

    def load_weights():
        for dest in range(nmp):
            w_load(dest).start()

    def pick(j):
        for g in range(chunk // GROUP):
            rows = pl.ds(g * GROUP, GROUP)
            picked = dot(choose_v[j], spread_v[:, rows, :].reshape(side, 2 * HEAD_DIM))
            send_v[j, :, rows, :] = picked.astype(BF16).reshape(n, GROUP, 2 * HEAD_DIM)

    def fetch():
        for peer in peers:
            pltpu.make_async_remote_copy(
                src_ref=table_v.at[me],
                dst_ref=table_v.at[me],
                send_sem=t_send,
                recv_sem=t_recv,
                device_id={"dp": peer},
                device_id_type=MESH,
            ).start()
        to_all(stage_v, spread_v, s1_send, s1_recv)
        load_weights()
        row = lax.broadcasted_iota(jnp.int32, (side, side), 0)
        col = lax.broadcasted_iota(jnp.int32, (side, side), 1)
        same = lax.rem(row, GROUP) == lax.rem(col, GROUP)
        prompt_of_col = jnp.where(same, col // GROUP, -1)
        others = table_v.at[pl.ds(0, n - 1)]
        pltpu.make_async_copy(others, others, t_recv).wait()

        for j in range(blocks):
            wanted = jnp.broadcast_to(table_v[:, j : j + 1, :], (n, GROUP, HEAD_DIM))
            wanted = wanted.reshape(side, HEAD_DIM)
            if side > HEAD_DIM:
                wanted = jnp.concatenate([wanted] * (side // HEAD_DIM), axis=1)
            else:
                wanted = wanted[:, :side]
            choose_v[j] = jnp.where(wanted == prompt_of_col, 1.0, 0.0).astype(BF16)

        pltpu.make_async_copy(spread_v, spread_v, s1_recv).wait()
        for j in range(blocks):
            pick(j)
            if j == 0:
                to_all(send_v.at[j], pre_v.at[j], s2_send.at[j], s2_recv.at[j])

    def part_of(j, t, cols):
        if t == tiles:
            return own_v[j, :, cols]
        got = pre_v[j, t * per_tile : (t + 1) * per_tile, :, cols]
        return got.reshape(block, HEAD_DIM)

    def visible(j):
        place = lax.broadcasted_iota(jnp.int32, (block, block), 1)
        key = lax.broadcasted_iota(jnp.int32, (block, block), 0)
        end = lengths_ref[j, 0]
        first = jnp.where(place >= end, end, 0)
        for s in range(1, lengths_ref.shape[1] - 1):
            end = end + lengths_ref[j, s]
            first = jnp.where(place >= end, end, first)
        return (key >= first) & (key <= place)

    def prepare(j):
        for copy in own_loads(j):
            copy.wait()
        pltpu.make_async_copy(pre_v.at[j], pre_v.at[j], s2_recv.at[j]).wait()
        if j + 1 < blocks:
            to_all(send_v.at[j + 1], pre_v.at[j + 1], s2_send.at[j + 1], s2_recv.at[j + 1])
        for t in range(tiles + 1):
            keys_t[:, t * block : (t + 1) * block] = part_of(j, t, key_cols).T
        grad_v[...] = jnp.zeros_like(grad_v)
        mask_v[...] = jnp.where(visible(j), 0.0, -1e30)

    def attend(j, lower, upper):
        per = 4

        def scores(h, slot):
            cols = pl.ds(pl.multiple_of(h * HEAD_DIM, HEAD_DIM), HEAD_DIM)
            qh = q_v[j, :, cols]
            top = None
            for t in range(tiles + 1):
                s = dot_nt(part_of(j, t, key_cols), qh)
                if t == tiles:
                    s = s + mask_v[...]
                score_v[slot, t] = s
                got = fold(s, jnp.max)
                top = got if top is None else jnp.maximum(top, got)
            return jnp.max(top, axis=0, keepdims=True)

        def middle(h, slot, top):
            cols = pl.ds(pl.multiple_of(h * HEAD_DIM, HEAD_DIM), HEAD_DIM)
            doh = do_v[j, :, cols]
            total = jnp.zeros((8, block), F32)
            mixed = jnp.zeros((8, block), F32)
            for t in range(tiles + 1):
                dp = dot_nt(part_of(j, t, value_cols), doh)
                dprob_v[slot, t] = dp
                e = jnp.exp2((score_v[slot, t] - top) * (SCALE * LOG2E))
                score_v[slot, t] = e
                total += fold(e, jnp.sum)
                mixed += fold(e * dp, jnp.sum)
            inverse = 1.0 / jnp.sum(total, axis=0, keepdims=True)
            delta = jnp.sum(mixed, axis=0, keepdims=True) * inverse
            return inverse, delta

        def grads(hs, stats):
            colss = [pl.ds(pl.multiple_of(h * HEAD_DIM, HEAD_DIM), HEAD_DIM) for h in hs]
            qs = jnp.concatenate([q_v[j, :, c] for c in colss], axis=0)
            dos = jnp.concatenate([do_v[j, :, c] for c in colss], axis=0)
            dqs = [jnp.zeros((HEAD_DIM, block), F32) for _ in hs]
            for t in range(tiles + 1):
                dss, ps = [], []
                for slot, (inverse, delta) in enumerate(stats):
                    prob = score_v[slot, t] * inverse
                    ds = (prob * (dprob_v[slot, t] - delta)).astype(BF16)
                    dss.append(ds)
                    ps.append(prob.astype(BF16))
                    dqs[slot] += dot(keys_t[:, t * block : (t + 1) * block], ds)
                grad_v[t, :, key_cols] += dot(jnp.concatenate(dss, axis=1), qs)
                grad_v[t, :, value_cols] += dot(jnp.concatenate(ps, axis=1), dos)
            for c, dq in zip(colss, dqs):
                qg_v[j, c, :] = (dq * SCALE).astype(BF16)

        def step(i, carry):
            hs = [i * per + s for s in range(per)]
            tops = [scores(h, s) for s, h in enumerate(hs)]
            stats = [middle(h, s, top) for s, (h, top) in enumerate(zip(hs, tops))]
            grads(hs, stats)
            return carry

        lax.fori_loop(lower // per, upper // per, step, 0)

    def rounded(t):
        return jnp.concatenate(
            [grad_v[t, :, key_cols] * SCALE, grad_v[t, :, value_cols]], axis=1
        ).astype(BF16)

    def give_back(j):
        for t in range(tiles):
            back_v[j, t * per_tile : (t + 1) * per_tile] = rounded(t).reshape(
                per_tile, chunk, 2 * HEAD_DIM
            )
        ownout_v[j] = rounded(tiles)
        pltpu.make_async_copy(
            ownout_v.at[j], own_hbm.at[pl.ds(j * block, block)], out_sem.at[j, 0]
        ).start()

        to_all(back_v.at[j], gather_v.at[j], b_send.at[j], b_recv.at[j])

    def bring_home():
        for j in range(blocks):
            pltpu.make_async_copy(gather_v.at[j], gather_v.at[j], b_recv.at[j]).wait()
        chosen = [choose_v[j].astype(F32).T.astype(BF16) for j in range(blocks)]
        for g in range(chunk // GROUP):
            rows = pl.ds(g * GROUP, GROUP)
            added = jnp.zeros((side, 2 * HEAD_DIM), F32)
            for j in range(blocks):
                added += dot(chosen[j], gather_v[j, :, rows, :].reshape(side, 2 * HEAD_DIM))
            home_v[:, rows, :] = added.astype(BF16).reshape(n, GROUP, 2 * HEAD_DIM)

        to_all(home_v, pre_hbm, h_send, h_recv)

    def project(j, dest):
        if j == 0:
            w_load(dest).wait()
        step = min(512, width)

        def tile(i, carry):
            rows = pl.ds(pl.multiple_of(i * step, step), step)
            from_w = pl.ds(pl.multiple_of(dest * width + i * step, step), step)
            part_v[j, dest, rows, :] = dot(w_v[from_w, :], qg_v[j]).astype(BF16)
            return carry

        lax.fori_loop(0, width // step, tile, 0)

    def to_sibling(j, y_dest, slot):
        return pltpu.make_async_remote_copy(
            src_ref=part_v.at[j, y_dest * 2 + 1 - core],
            dst_ref=sib_v.at[j, slot],
            send_sem=sib_send.at[j, slot],
            recv_sem=sib_recv.at[j, slot],
            device_id={"mp": sibling},
            device_id_type=MESH,
        )

    def remote(src, dst, send, recv, dest):
        return pltpu.make_async_remote_copy(
            src_ref=src,
            dst_ref=dst,
            send_sem=send,
            recv_sem=recv,
            device_id={"mp": dest},
            device_id_type=MESH,
        )

    halves, ways = (pl.ds(0, half), pl.ds(half, half)), (right, left)
    pieces = 2
    piece = half // pieces

    def piece_rows(way, p):
        return pl.ds(way * half + p * piece, piece)

    def opposite(j, way, p):
        src = part_v.at[j, y_opp * 2 + core, piece_rows(way, p)]
        sems = opp_send.at[j, way, p], opp_recv.at[j, way, p]
        return remote(src, hop_v.at[j, way, pl.ds(p * piece, piece)], *sems, ways[way])

    def raw(j, way):
        rows = halves[1 - way]
        src, dst = part_v.at[j, ways[way], rows], side_v.at[j, way, rows]
        return remote(src, dst, raw_send.at[j, way], raw_recv.at[j, way], ways[way])

    def mixed(j, way, p):
        rows = piece_rows(way, p)
        src, dst = part_v.at[j, ways[way], rows], side_v.at[j, way, rows]
        return remote(src, dst, mix_send.at[j, way, p], mix_recv.at[j, way, p], ways[way])

    def add_sibling(j, y_dest, slot):
        mine = part_v[j, y_dest * 2 + core].astype(F32)
        part_v[j, y_dest * 2 + core] = (mine + sib_v[j, slot].astype(F32)).astype(BF16)

    def send_partials(j):
        project(j, y_opp * 2 + 1 - core)
        to_sibling(j, y_opp, 0).start()
        project(j, y_opp * 2 + core)
        project(j, y_right * 2 + 1 - core)
        to_sibling(j, y_right, 1).start()
        to_sibling(j, y_opp, 0).wait_recv()
        add_sibling(j, y_opp, 0)
        for p in range(pieces):
            for way in range(2):
                opposite(j, way, p).start()
        project(j, y_left * 2 + 1 - core)
        to_sibling(j, y_left, 2).start()
        project(j, y_right * 2 + core)
        project(j, y_left * 2 + core)
        to_sibling(j, y_right, 1).wait_recv()
        add_sibling(j, y_right, 1)
        raw(j, 0).start()
        project(j, y * 2 + 1 - core)
        to_sibling(j, y, 3).start()
        to_sibling(j, y_left, 2).wait_recv()
        add_sibling(j, y_left, 2)
        raw(j, 1).start()
        project(j, y * 2 + core)

    def pass_on(j, p):
        for way in range(2):
            opposite(j, way, p).wait_recv()
            rows = piece_rows(way, p)
            hop = hop_v[j, way, pl.ds(p * piece, piece), :].astype(F32)
            part_v[j, ways[way], rows, :] = (
                part_v[j, ways[way], rows, :].astype(F32) + hop
            ).astype(BF16)
            mixed(j, way, p).start()

    def out_copy(j, way, p):
        cols = piece_rows(way, p)
        rows = pl.ds(j * block, block)
        return pltpu.make_async_copy(
            sum_v.at[j, :, cols], out_hbm.at[rows, cols], out_sem.at[j, 1 + way * pieces + p]
        )

    def finish(j):
        to_sibling(j, y, 3).wait_recv()
        for way in range(2):
            raw(j, way).wait_recv()
        for p in range(pieces):
            for way in range(2):
                rows = piece_rows(way, p)
                added = part_v[j, y * 2 + core, rows, :].astype(F32)
                added += sib_v[j, 3, rows, :].astype(F32)
                added += side_v[j, 1 - way, rows, :].astype(F32)
                mixed(j, way, p).wait_recv()
                added += side_v[j, way, rows, :].astype(F32)
                sum_v[j, :, rows] = added.astype(BF16).T
                out_copy(j, way, p).start()

    def all_but_one(ref, sem):
        part = ref.at[pl.ds(0, n - 1)]
        pltpu.make_async_copy(part, part, sem).wait()

    def end_fetch():
        all_but_one(table_v, t_send)
        all_but_one(spread_v, s1_send)
        for j in range(blocks):
            all_but_one(send_v.at[j], s2_send.at[j])

    def end_back():
        all_but_one(home_v, h_send)
        for j in range(blocks):
            all_but_one(back_v.at[j], b_send.at[j])
            pltpu.make_async_copy(
                ownout_v.at[j], own_hbm.at[pl.ds(j * block, block)], out_sem.at[j, 0]
            ).wait()
        pltpu.make_async_copy(pre_hbm, pre_hbm, h_recv).wait()

    def end_sum(j):
        for slot, y_dest in enumerate((y_opp, y_right, y_left, y)):
            to_sibling(j, y_dest, slot).wait_send()
        for way in range(2):
            raw(j, way).wait_send()
            for p in range(pieces):
                opposite(j, way, p).wait_send()
                mixed(j, way, p).wait_send()
                out_copy(j, way, p).wait()

    fetch()
    prepare(0)
    attend(0, 0, heads)
    give_back(0)
    send_partials(0)
    prepare(1)
    attend(1, 0, heads // 2)
    pass_on(0, 0)
    pass_on(0, 1)
    attend(1, heads // 2, heads)
    give_back(1)
    send_partials(1)
    finish(0)
    bring_home()
    pass_on(1, 0)
    pass_on(1, 1)
    finish(1)
    end_fetch()
    end_back()
    for j in range(blocks):
        end_sum(j)


def results(out, own, pre, input_grad, key_grad, value_grad, pre_key_grad, pre_value_grad, *held):
    out_v, own_v, pre_v, load_sem, store_sem = held
    keys, values = pl.ds(0, HEAD_DIM), pl.ds(HEAD_DIM, HEAD_DIM)
    half = out.shape[0] // 2
    upper, lower = pl.ds(0, half), pl.ds(half, half)
    loads = [(out.at[r], out_v.at[r]) for r in (upper, lower)] + [(own, own_v), (pre, pre_v)]
    stores = [
        [(out_v.at[upper], input_grad.at[upper])],
        [(out_v.at[lower], input_grad.at[lower])],
        [(own_v.at[:, keys], key_grad), (own_v.at[:, values], value_grad)],
        [(pre_v.at[:, keys], pre_key_grad), (pre_v.at[:, values], pre_value_grad)],
    ]
    loads = [pltpu.make_async_copy(a, b, load_sem.at[i]) for i, (a, b) in enumerate(loads)]
    for copy in loads:
        copy.start()
    started = []
    for load, pairs in zip(loads, stores):
        load.wait()
        for a, b in pairs:
            copy = pltpu.make_async_copy(a, b, store_sem.at[len(started)])
            copy.start()
            started.append(copy)
    for copy in started:
        copy.wait()


def shards(
    queries,
    out_grad,
    response_keys,
    response_values,
    prefix_keys,
    prefix_values,
    q_weight,
    block_prompt,
    response_lengths,
):
    n, nmp = lax.axis_size("dp"), lax.axis_size("mp")
    blocks = block_prompt.shape[0]
    rows, cols = queries.shape
    block = rows // blocks
    prefix = prefix_keys.shape[0]
    chunk = prefix // n
    tiles = prefix // block
    width = q_weight.shape[0] // nmp
    two = 2 * HEAD_DIM
    dma = pltpu.SemaphoreType.DMA
    any_space = pl.BlockSpec(memory_space=pl.ANY)
    smem = pl.BlockSpec(memory_space=pltpu.SMEM)
    flops = 2 * rows * cols * (5 * (prefix + block) + q_weight.shape[0])
    out, own, pre = pl.pallas_call(
        functools.partial(kernel, n, nmp),
        out_shape=(
            jax.ShapeDtypeStruct((rows, width), BF16),
            jax.ShapeDtypeStruct((rows, two), BF16),
            jax.ShapeDtypeStruct((n, chunk, two), BF16),
        ),
        in_specs=[smem, smem] + [any_space] * 7,
        out_specs=(any_space,) * 3,
        scratch_shapes=[
            pltpu.VMEM((blocks, block, cols), BF16),
            pltpu.VMEM((blocks, block, cols), BF16),
            pltpu.VMEM((blocks, block, two), BF16),
            pltpu.VMEM(q_weight.shape, BF16),
            pltpu.VMEM((n, blocks, HEAD_DIM), jnp.int32),
            pltpu.VMEM((n, chunk, two), BF16),
            pltpu.VMEM((n, chunk, two), BF16),
            pltpu.VMEM((blocks, n * GROUP, n * GROUP), BF16),
            pltpu.VMEM((blocks, n, chunk, two), BF16),
            pltpu.VMEM((blocks, n, chunk, two), BF16),
            pltpu.VMEM((HEAD_DIM, prefix + block), BF16),
            pltpu.VMEM((4, tiles + 1, block, block), F32),
            pltpu.VMEM((4, tiles + 1, block, block), F32),
            pltpu.VMEM((block, block), F32),
            pltpu.VMEM((tiles + 1, block, two), F32),
            pltpu.VMEM((blocks, cols, block), BF16),
            pltpu.VMEM((blocks, block, two), BF16),
            pltpu.VMEM((blocks, n, chunk, two), BF16),
            pltpu.VMEM((blocks, n, chunk, two), BF16),
            pltpu.VMEM((n, chunk, two), BF16),
            pltpu.VMEM((blocks, nmp, width, block), BF16),
            pltpu.VMEM((blocks, nmp // 2, width, block), BF16),
            pltpu.VMEM((blocks, 2, width // 2, block), BF16),
            pltpu.VMEM((blocks, 2, width, block), BF16),
            pltpu.VMEM((blocks, block, width), BF16),
            dma((blocks, 4)),
            dma((nmp,)),
            dma,
            dma,
            dma((2,)),
            dma,
            dma,
            dma((blocks,)),
            dma((blocks,)),
            dma((blocks,)),
            dma((blocks,)),
            dma,
            dma,
            dma((blocks, 4)),
            dma((blocks, 4)),
            dma((blocks, 2, 2)),
            dma((blocks, 2, 2)),
            dma((blocks, 2)),
            dma((blocks, 2)),
            dma((blocks, 2, 2)),
            dma((blocks, 2, 2)),
            dma((blocks, 5)),
        ],
        compiler_params=pltpu.CompilerParams(
            collective_id=0, has_side_effects=True, vmem_limit_bytes=60 * 2**20
        ),
        cost_estimate=pl.CostEstimate(
            flops=flops, bytes_accessed=2 * q_weight.size, transcendentals=0
        ),
        name="attention_backward",
    )(
        block_prompt,
        response_lengths,
        queries,
        out_grad,
        response_keys,
        response_values,
        prefix_keys.reshape(n, chunk, HEAD_DIM),
        prefix_values.reshape(n, chunk, HEAD_DIM),
        q_weight,
    )
    return pl.pallas_call(
        results,
        out_shape=(
            jax.ShapeDtypeStruct((rows, width), BF16),
            jax.ShapeDtypeStruct((rows, HEAD_DIM), BF16),
            jax.ShapeDtypeStruct((rows, HEAD_DIM), BF16),
            jax.ShapeDtypeStruct((prefix, HEAD_DIM), BF16),
            jax.ShapeDtypeStruct((prefix, HEAD_DIM), BF16),
        ),
        in_specs=[any_space] * 3,
        out_specs=(any_space,) * 5,
        scratch_shapes=[
            pltpu.VMEM((rows, width), BF16),
            pltpu.VMEM((rows, two), BF16),
            pltpu.VMEM((prefix, two), BF16),
            dma((4,)),
            dma((6,)),
        ],
        compiler_params=pltpu.CompilerParams(vmem_limit_bytes=60 * 2**20),
        name="results",
    )(out, own, pre.reshape(prefix, two))


def solution(mesh):
    return jax.shard_map(
        shards,
        mesh=mesh,
        in_specs=(
            P("dp", "mp"),
            P("dp", "mp"),
            P("dp", "mp"),
            P("dp", "mp"),
            P("dp", "mp"),
            P("dp", "mp"),
            P(None, "mp"),
            P("dp"),
            P("dp", None),
        ),
        out_specs=(P("dp", "mp"), P("dp", "mp"), P("dp", "mp"), P("dp", "mp"), P("dp", "mp")),
        check_vma=False,
    )
```

```python
import functools

import jax
import jax.numpy as jnp
from jax import lax
from jax.experimental import pallas as pl
from jax.experimental.pallas import tpu as pltpu
from jax.sharding import PartitionSpec as P

HEAD_DIM = 128
PER_SOFTEN = 4
PER_GRADS = 2
GROUP = 16
SCALE = HEAD_DIM ** (-0.5)
LOG2E = 1.4426950408889634
MESH = pl.DeviceIdType.MESH
F32 = jnp.float32
BF16 = jnp.bfloat16


def dot(a, b):
    return jnp.dot(a, b, preferred_element_type=F32)


def dot_nt(a, b):
    return lax.dot_general(a, b, (((1,), (1,)), ((), ())), preferred_element_type=F32)


def fold(x, op):
    rows, cols = x.shape
    return op(x.reshape(rows // 8, 8, cols), axis=0)


def kernel(
    n,
    nmp,
    prompt_ref,
    lengths_ref,
    q_hbm,
    do_hbm,
    rk_hbm,
    rv_hbm,
    pk_hbm,
    pv_hbm,
    w_hbm,
    out_hbm,
    own_hbm,
    pre_hbm,
    q_v,
    do_v,
    own_v,
    w_v,
    table_v,
    stage_v,
    spread_v,
    choose_v,
    send_v,
    pre_v,
    keys_t,
    score_v,
    dprob_v,
    mask_v,
    inverse_v,
    grad_v,
    qg_v,
    ownout_v,
    back_v,
    gather_v,
    home_v,
    part_v,
    sib_v,
    hop_v,
    side_v,
    in_sem,
    w_sem,
    t_send,
    t_recv,
    s1_sem,
    s1_send,
    s1_recv,
    s2_send,
    s2_recv,
    b_send,
    b_recv,
    h_send,
    h_recv,
    sib_send,
    sib_recv,
    opp_send,
    opp_recv,
    raw_send,
    raw_recv,
    mix_send,
    mix_recv,
    out_sem,
):
    me = lax.axis_index("dp")
    mp = lax.axis_index("mp")
    ny = nmp // 2
    y, core = mp // 2, lax.rem(mp, 2)
    y_right, y_left, y_opp = lax.rem(y + 1, ny), lax.rem(y + ny - 1, ny), lax.rem(y + 2, ny)
    right, left, sibling = y_right * 2 + core, y_left * 2 + core, y * 2 + 1 - core
    blocks, block = q_v.shape[0], q_v.shape[1]
    chunk = send_v.shape[3]
    width = sib_v.shape[2]
    half = width // 2
    heads = q_v.shape[2] // HEAD_DIM
    tiles = score_v.shape[1] - 1
    per_tile = n // tiles

    def load(j, what, src, dst):
        return pltpu.make_async_copy(src, dst, in_sem.at[j, what])

    def own_loads(j):
        rows = pl.ds(j * block, block)
        return [
            load(j, 0, q_hbm.at[rows], q_v.at[j]),
            load(j, 1, do_hbm.at[rows], do_v.at[j]),
            load(j, 2, rk_hbm.at[rows], own_v.at[j, :, pl.ds(0, HEAD_DIM)]),
            load(j, 3, rv_hbm.at[rows], own_v.at[j, :, pl.ds(HEAD_DIM, HEAD_DIM)]),
        ]

    def w_load(dest):
        rows = pl.ds(pl.multiple_of(dest * width, width), width)
        return pltpu.make_async_copy(w_hbm.at[rows], w_v.at[rows], w_sem.at[dest])

    key_cols, value_cols = pl.ds(0, HEAD_DIM), pl.ds(HEAD_DIM, HEAD_DIM)
    side = n * GROUP

    def prompt_loads():
        return [
            pltpu.make_async_copy(src, stage_v.at[:, what], s1_sem.at[what])
            for what, src in enumerate((pk_hbm, pv_hbm))
        ]

    for copy in prompt_loads():
        copy.start()
    for j in range(blocks):
        for copy in own_loads(j):
            copy.start()

    side_x = 4 if n == 16 else n
    if n == 16:
        ones = [(0, 1), (0, 3), (1, 0), (3, 0), (1, 1), (3, 3), (1, 3), (3, 1)]
        offsets = ones + [(0, 2), (2, 0), (1, 2), (3, 2), (2, 1), (2, 3), (2, 2)]
    else:
        offsets = [(0, o) for o in range(1, n)]
    side_z = n // side_x
    my_z, my_x = me // side_x, lax.rem(me, side_x)
    peers = [
        lax.rem(my_z + dz, side_z) * side_x + lax.rem(my_x + dx, side_x) for dz, dx in offsets
    ]

    barrier = pltpu.get_barrier_semaphore()
    for peer in peers:
        pl.semaphore_signal(barrier, inc=1, device_id={"dp": peer}, device_id_type=MESH)
    for other in (right, left, sibling):
        pl.semaphore_signal(barrier, inc=1, device_id={"mp": other}, device_id_type=MESH)
    for j in range(blocks):
        table_v[me, j, :] = jnp.full((HEAD_DIM,), prompt_ref[j], jnp.int32)
    for copy in prompt_loads():
        copy.wait()
    pl.semaphore_wait(barrier, n - 1 + 3)

    def to_all(src, dst, send, recv):
        for peer in peers:
            pltpu.make_async_remote_copy(
                src_ref=src.at[peer],
                dst_ref=dst.at[me],
                send_sem=send,
                recv_sem=recv,
                device_id={"dp": peer},
                device_id_type=MESH,
            ).start()
        pltpu.make_async_copy(src.at[me], dst.at[me], recv).start()

    def load_weights():
        for dest in range(nmp):
            w_load(dest).start()

    def pick(j, what):
        for g in range(chunk // GROUP):
            rows = pl.ds(g * GROUP, GROUP)
            picked = dot(choose_v[j], spread_v[:, what, rows, :].reshape(side, HEAD_DIM))
            send_v[j, :, what, rows, :] = picked.astype(BF16).reshape(n, GROUP, HEAD_DIM)

    def hand_out(j, what):
        to_all(
            send_v.at[j, :, what], pre_v.at[j, :, what], s2_send.at[j, what], s2_recv.at[j, what]
        )

    def arrived(ref, sem):
        pltpu.make_async_copy(ref, ref, sem).wait()

    def fetch():
        for peer in peers:
            pltpu.make_async_remote_copy(
                src_ref=table_v.at[me],
                dst_ref=table_v.at[me],
                send_sem=t_send,
                recv_sem=t_recv,
                device_id={"dp": peer},
                device_id_type=MESH,
            ).start()
        for what in range(2):
            to_all(stage_v.at[:, what], spread_v.at[:, what], s1_send.at[what], s1_recv.at[what])
        load_weights()
        row = lax.broadcasted_iota(jnp.int32, (side, side), 0)
        col = lax.broadcasted_iota(jnp.int32, (side, side), 1)
        same = lax.rem(row, GROUP) == lax.rem(col, GROUP)
        prompt_of_col = jnp.where(same, col // GROUP, -1)
        arrived(table_v.at[pl.ds(0, n - 1)], t_recv)

        for j in range(blocks):
            wanted = jnp.broadcast_to(table_v[:, j : j + 1, :], (n, GROUP, HEAD_DIM))
            wanted = wanted.reshape(side, HEAD_DIM)
            if side > HEAD_DIM:
                wanted = jnp.concatenate([wanted] * (side // HEAD_DIM), axis=1)
            else:
                wanted = wanted[:, :side]
            choose_v[j] = jnp.where(wanted == prompt_of_col, 1.0, 0.0).astype(BF16)

        for what in range(2):
            arrived(spread_v.at[:, what], s1_recv.at[what])
            pick(0, what)
            hand_out(0, what)
        for j in range(1, blocks):
            for what in range(2):
                pick(j, what)

    def part_of(j, t, what):
        if t == tiles:
            return own_v[j, :, (key_cols, value_cols)[what]]
        return pre_v[j, t * per_tile : (t + 1) * per_tile, what].reshape(block, HEAD_DIM)

    def visible(j):
        place = lax.broadcasted_iota(jnp.int32, (block, block), 1)
        key = lax.broadcasted_iota(jnp.int32, (block, block), 0)
        end = lengths_ref[j, 0]
        first = jnp.where(place >= end, end, 0)
        for s in range(1, lengths_ref.shape[1] - 1):
            end = end + lengths_ref[j, s]
            first = jnp.where(place >= end, end, first)
        return (key >= first) & (key <= place)

    def wait_keys(j):
        for copy in own_loads(j):
            copy.wait()
        arrived(pre_v.at[j, :, 0], s2_recv.at[j, 0])

    def wait_values(j):
        arrived(pre_v.at[j, :, 1], s2_recv.at[j, 1])

    def head_cols(h):
        return pl.ds(pl.multiple_of(h * HEAD_DIM, HEAD_DIM), HEAD_DIM)

    def soften(j):
        mask_v[...] = jnp.where(visible(j), 0.0, -1e30)
        for t in range(tiles + 1):
            keys_t[:, t * block : (t + 1) * block] = part_of(j, t, 0).T

        def scores(h):
            qh = q_v[j, :, head_cols(h)]
            top = None
            for t in range(tiles + 1):
                s = dot_nt(part_of(j, t, 0), qh)
                if t == tiles:
                    s = s + mask_v[...]
                score_v[h, t] = s
                got = fold(s, jnp.max)
                top = got if top is None else jnp.maximum(top, got)
            return jnp.max(top, axis=0, keepdims=True)

        def powers(h, top):
            total = jnp.zeros((8, block), F32)
            for t in range(tiles + 1):
                e = jnp.exp2((score_v[h, t] - top) * (SCALE * LOG2E))
                score_v[h, t] = e
                total += fold(e, jnp.sum)
            inverse = 1.0 / jnp.sum(total, axis=0, keepdims=True)
            inverse_v[h] = jnp.broadcast_to(inverse, (8, block))

        per = PER_SOFTEN

        def step(i, carry):
            hs = [i * per + s for s in range(per)]
            tops = [scores(h) for h in hs]
            for h, top in zip(hs, tops):
                powers(h, top)
            return carry

        lax.fori_loop(0, heads // per, step, 0)

    def attend(j, lower, upper):
        def middle(h, slot):
            doh = do_v[j, :, head_cols(h)]
            mixed = jnp.zeros((8, block), F32)
            for t in range(tiles + 1):
                dp = dot_nt(part_of(j, t, 1), doh)
                dprob_v[slot, t] = dp
                mixed += fold(score_v[h, t] * dp, jnp.sum)
            inverse = inverse_v[h, 0:1, :]
            return inverse, jnp.sum(mixed, axis=0, keepdims=True) * inverse

        def grads(hs, stats):
            qs = jnp.concatenate([q_v[j, :, head_cols(h)] for h in hs], axis=0)
            dos = jnp.concatenate([do_v[j, :, head_cols(h)] for h in hs], axis=0)
            dqs = [jnp.zeros((HEAD_DIM, block), F32) for _ in hs]
            for t in range(tiles + 1):
                dss, ps = [], []
                for slot, (inverse, delta) in enumerate(stats):
                    prob = score_v[hs[slot], t] * inverse
                    ds = (prob * (dprob_v[slot, t] - delta)).astype(BF16)
                    dss.append(ds)
                    ps.append(prob.astype(BF16))
                    dqs[slot] += dot(keys_t[:, t * block : (t + 1) * block], ds)
                grad_v[t, :, key_cols] += dot(jnp.concatenate(dss, axis=1), qs)
                grad_v[t, :, value_cols] += dot(jnp.concatenate(ps, axis=1), dos)
            for h, dq in zip(hs, dqs):
                qg_v[j, head_cols(h), :] = (dq * SCALE).astype(BF16)

        per = PER_GRADS

        def step(i, carry):
            hs = [i * per + s for s in range(per)]
            grads(hs, [middle(h, s) for s, h in enumerate(hs)])
            return carry

        if lower == 0:
            grad_v[...] = jnp.zeros_like(grad_v)
        lax.fori_loop(lower // per, upper // per, step, 0)

    def rounded(t):
        return jnp.concatenate(
            [grad_v[t, :, key_cols] * SCALE, grad_v[t, :, value_cols]], axis=1
        ).astype(BF16)

    def give_back(j):
        for t in range(tiles):
            back_v[j, t * per_tile : (t + 1) * per_tile] = rounded(t).reshape(
                per_tile, chunk, 2 * HEAD_DIM
            )
        ownout_v[j] = rounded(tiles)
        pltpu.make_async_copy(
            ownout_v.at[j], own_hbm.at[pl.ds(j * block, block)], out_sem.at[j, 0]
        ).start()

        to_all(back_v.at[j], gather_v.at[j], b_send.at[j], b_recv.at[j])

    def bring_home():
        for j in range(blocks):
            pltpu.make_async_copy(gather_v.at[j], gather_v.at[j], b_recv.at[j]).wait()
        chosen = [choose_v[j].astype(F32).T.astype(BF16) for j in range(blocks)]
        for g in range(chunk // GROUP):
            rows = pl.ds(g * GROUP, GROUP)
            added = jnp.zeros((side, 2 * HEAD_DIM), F32)
            for j in range(blocks):
                added += dot(chosen[j], gather_v[j, :, rows, :].reshape(side, 2 * HEAD_DIM))
            home_v[:, rows, :] = added.astype(BF16).reshape(n, GROUP, 2 * HEAD_DIM)

        to_all(home_v, pre_hbm, h_send, h_recv)

    def project(j, dest, first=0, last=2):
        if j == 0 and first == 0:
            w_load(dest).wait()
        step = width // 2

        def tile(i, carry):
            rows = pl.ds(pl.multiple_of(i * step, step), step)
            from_w = pl.ds(pl.multiple_of(dest * width + i * step, step), step)
            part_v[j, dest, rows, :] = dot(w_v[from_w, :], qg_v[j]).astype(BF16)
            return carry

        lax.fori_loop(first, last, tile, 0)

    def to_sibling(j, y_dest, slot):
        return pltpu.make_async_remote_copy(
            src_ref=part_v.at[j, y_dest * 2 + 1 - core],
            dst_ref=sib_v.at[j, slot],
            send_sem=sib_send.at[j, slot],
            recv_sem=sib_recv.at[j, slot],
            device_id={"mp": sibling},
            device_id_type=MESH,
        )

    def remote(src, dst, send, recv, dest):
        return pltpu.make_async_remote_copy(
            src_ref=src,
            dst_ref=dst,
            send_sem=send,
            recv_sem=recv,
            device_id={"mp": dest},
            device_id_type=MESH,
        )

    halves, ways = (pl.ds(0, half), pl.ds(half, half)), (right, left)
    pieces = 2
    piece = half // pieces

    def piece_rows(way, p):
        return pl.ds(way * half + p * piece, piece)

    def opposite(j, way, p):
        src = part_v.at[j, y_opp * 2 + core, piece_rows(way, p)]
        sems = opp_send.at[j, way, p], opp_recv.at[j, way, p]
        return remote(src, hop_v.at[j, way, pl.ds(p * piece, piece)], *sems, ways[way])

    def raw(j, way):
        rows = halves[1 - way]
        src, dst = part_v.at[j, ways[way], rows], side_v.at[j, way, rows]
        return remote(src, dst, raw_send.at[j, way], raw_recv.at[j, way], ways[way])

    def mixed(j, way, p):
        rows = piece_rows(way, p)
        src, dst = part_v.at[j, ways[way], rows], side_v.at[j, way, rows]
        return remote(src, dst, mix_send.at[j, way, p], mix_recv.at[j, way, p], ways[way])

    def add_sibling(j, y_dest, slot):
        mine = part_v[j, y_dest * 2 + core].astype(F32)
        part_v[j, y_dest * 2 + core] = (mine + sib_v[j, slot].astype(F32)).astype(BF16)

    def send_partials(j):
        project(j, y_opp * 2 + 1 - core)
        to_sibling(j, y_opp, 0).start()
        project(j, y_opp * 2 + core)
        project(j, y_right * 2 + 1 - core)
        to_sibling(j, y_right, 1).start()
        to_sibling(j, y_opp, 0).wait_recv()
        add_sibling(j, y_opp, 0)
        for p in range(pieces):
            for way in range(2):
                opposite(j, way, p).start()
        give_back(j)
        project(j, y_left * 2 + 1 - core)
        to_sibling(j, y_left, 2).start()
        project(j, y_right * 2 + core)
        project(j, y_left * 2 + core)
        to_sibling(j, y_right, 1).wait_recv()
        add_sibling(j, y_right, 1)
        raw(j, 0).start()
        project(j, y * 2 + 1 - core)
        to_sibling(j, y, 3).start()
        to_sibling(j, y_left, 2).wait_recv()
        add_sibling(j, y_left, 2)
        raw(j, 1).start()
        project(j, y * 2 + core)

    def pass_on(j, p):
        for way in range(2):
            opposite(j, way, p).wait_recv()
            rows = piece_rows(way, p)
            hop = hop_v[j, way, pl.ds(p * piece, piece), :].astype(F32)
            part_v[j, ways[way], rows, :] = (
                part_v[j, ways[way], rows, :].astype(F32) + hop
            ).astype(BF16)
            mixed(j, way, p).start()

    def out_copy(j, way, p):
        cols = piece_rows(way, p)
        rows = pl.ds(j * block, block)
        return pltpu.make_async_copy(
            q_v.at[j, :, cols], out_hbm.at[rows, cols], out_sem.at[j, 1 + way * pieces + p]
        )

    def finish(j):
        to_sibling(j, y, 3).wait_recv()
        for way in range(2):
            raw(j, way).wait_recv()
        for p in range(pieces):
            for way in range(2):
                rows = piece_rows(way, p)
                added = part_v[j, y * 2 + core, rows, :].astype(F32)
                added += sib_v[j, 3, rows, :].astype(F32)
                added += side_v[j, 1 - way, rows, :].astype(F32)
                mixed(j, way, p).wait_recv()
                added += side_v[j, way, rows, :].astype(F32)
                q_v[j, :, rows] = added.astype(BF16).T
                out_copy(j, way, p).start()

    def all_but_one(ref, sem):
        part = ref.at[pl.ds(0, n - 1)]
        pltpu.make_async_copy(part, part, sem).wait()

    def end_fetch():
        all_but_one(table_v, t_send)
        for what in range(2):
            all_but_one(spread_v.at[:, what], s1_send.at[what])
            for j in range(blocks):
                all_but_one(send_v.at[j, :, what], s2_send.at[j, what])

    def end_back():
        all_but_one(home_v, h_send)
        for j in range(blocks):
            all_but_one(back_v.at[j], b_send.at[j])
            pltpu.make_async_copy(
                ownout_v.at[j], own_hbm.at[pl.ds(j * block, block)], out_sem.at[j, 0]
            ).wait()
        pltpu.make_async_copy(pre_hbm, pre_hbm, h_recv).wait()

    def end_sum(j):
        for slot, y_dest in enumerate((y_opp, y_right, y_left, y)):
            to_sibling(j, y_dest, slot).wait_send()
        for way in range(2):
            raw(j, way).wait_send()
            for p in range(pieces):
                opposite(j, way, p).wait_send()
                mixed(j, way, p).wait_send()
                out_copy(j, way, p).wait()

    fetch()
    wait_keys(0)
    soften(0)
    wait_values(0)
    for what in range(2):
        hand_out(1, what)
    attend(0, 0, heads)
    send_partials(0)
    wait_keys(1)
    wait_values(1)
    soften(1)
    pass_on(0, 0)
    pass_on(0, 1)
    attend(1, 0, heads)
    send_partials(1)
    pass_on(1, 0)
    finish(0)
    pass_on(1, 1)
    bring_home()
    finish(1)
    end_fetch()
    end_back()
    for j in range(blocks):
        end_sum(j)


def results(out, own, pre, input_grad, key_grad, value_grad, pre_key_grad, pre_value_grad, *held):
    out_v, own_v, pre_v, load_sem, store_sem = held
    keys, values = pl.ds(0, HEAD_DIM), pl.ds(HEAD_DIM, HEAD_DIM)
    half = out.shape[0] // 2
    upper, lower = pl.ds(0, half), pl.ds(half, half)
    loads = [(out.at[r], out_v.at[r]) for r in (upper, lower)] + [(own, own_v), (pre, pre_v)]
    stores = [
        [(out_v.at[upper], input_grad.at[upper])],
        [(out_v.at[lower], input_grad.at[lower])],
        [(own_v.at[:, keys], key_grad), (own_v.at[:, values], value_grad)],
        [(pre_v.at[:, keys], pre_key_grad), (pre_v.at[:, values], pre_value_grad)],
    ]
    loads = [pltpu.make_async_copy(a, b, load_sem.at[i]) for i, (a, b) in enumerate(loads)]
    for copy in loads:
        copy.start()
    started = []
    for load, pairs in zip(loads, stores):
        load.wait()
        for a, b in pairs:
            copy = pltpu.make_async_copy(a, b, store_sem.at[len(started)])
            copy.start()
            started.append(copy)
    for copy in started:
        copy.wait()


def shards(
    queries,
    out_grad,
    response_keys,
    response_values,
    prefix_keys,
    prefix_values,
    q_weight,
    block_prompt,
    response_lengths,
):
    n, nmp = lax.axis_size("dp"), lax.axis_size("mp")
    blocks = block_prompt.shape[0]
    rows, cols = queries.shape
    block = rows // blocks
    prefix = prefix_keys.shape[0]
    chunk = prefix // n
    tiles = prefix // block
    width = q_weight.shape[0] // nmp
    two = 2 * HEAD_DIM
    dma = pltpu.SemaphoreType.DMA
    any_space = pl.BlockSpec(memory_space=pl.ANY)
    smem = pl.BlockSpec(memory_space=pltpu.SMEM)
    flops = 2 * rows * cols * (5 * (prefix + block) + q_weight.shape[0])
    out, own, pre = pl.pallas_call(
        functools.partial(kernel, n, nmp),
        out_shape=(
            jax.ShapeDtypeStruct((rows, width), BF16),
            jax.ShapeDtypeStruct((rows, two), BF16),
            jax.ShapeDtypeStruct((n, chunk, two), BF16),
        ),
        in_specs=[smem, smem] + [any_space] * 7,
        out_specs=(any_space,) * 3,
        scratch_shapes=[
            pltpu.VMEM((blocks, block, cols), BF16),
            pltpu.VMEM((blocks, block, cols), BF16),
            pltpu.VMEM((blocks, block, two), BF16),
            pltpu.VMEM(q_weight.shape, BF16),
            pltpu.VMEM((n, blocks, HEAD_DIM), jnp.int32),
            pltpu.VMEM((n, 2, chunk, HEAD_DIM), BF16),
            pltpu.VMEM((n, 2, chunk, HEAD_DIM), BF16),
            pltpu.VMEM((blocks, n * GROUP, n * GROUP), BF16),
            pltpu.VMEM((blocks, n, 2, chunk, HEAD_DIM), BF16),
            pltpu.VMEM((blocks, n, 2, chunk, HEAD_DIM), BF16),
            pltpu.VMEM((HEAD_DIM, prefix + block), BF16),
            pltpu.VMEM((cols // HEAD_DIM, tiles + 1, block, block), F32),
            pltpu.VMEM((PER_GRADS, tiles + 1, block, block), F32),
            pltpu.VMEM((block, block), F32),
            pltpu.VMEM((cols // HEAD_DIM, 8, block), F32),
            pltpu.VMEM((tiles + 1, block, two), F32),
            pltpu.VMEM((blocks, cols, block), BF16),
            pltpu.VMEM((blocks, block, two), BF16),
            pltpu.VMEM((blocks, n, chunk, two), BF16),
            pltpu.VMEM((blocks, n, chunk, two), BF16),
            pltpu.VMEM((n, chunk, two), BF16),
            pltpu.VMEM((blocks, nmp, width, block), BF16),
            pltpu.VMEM((blocks, nmp // 2, width, block), BF16),
            pltpu.VMEM((blocks, 2, width // 2, block), BF16),
            pltpu.VMEM((blocks, 2, width, block), BF16),
            dma((blocks, 4)),
            dma((nmp,)),
            dma,
            dma,
            dma((2,)),
            dma((2,)),
            dma((2,)),
            dma((blocks, 2)),
            dma((blocks, 2)),
            dma((blocks,)),
            dma((blocks,)),
            dma,
            dma,
            dma((blocks, 4)),
            dma((blocks, 4)),
            dma((blocks, 2, 2)),
            dma((blocks, 2, 2)),
            dma((blocks, 2)),
            dma((blocks, 2)),
            dma((blocks, 2, 2)),
            dma((blocks, 2, 2)),
            dma((blocks, 5)),
        ],
        compiler_params=pltpu.CompilerParams(
            collective_id=0, has_side_effects=True, vmem_limit_bytes=60 * 2**20
        ),
        cost_estimate=pl.CostEstimate(
            flops=flops, bytes_accessed=2 * q_weight.size, transcendentals=0
        ),
        name="attention_backward",
    )(
        block_prompt,
        response_lengths,
        queries,
        out_grad,
        response_keys,
        response_values,
        prefix_keys.reshape(n, chunk, HEAD_DIM),
        prefix_values.reshape(n, chunk, HEAD_DIM),
        q_weight,
    )
    return pl.pallas_call(
        results,
        out_shape=(
            jax.ShapeDtypeStruct((rows, width), BF16),
            jax.ShapeDtypeStruct((rows, HEAD_DIM), BF16),
            jax.ShapeDtypeStruct((rows, HEAD_DIM), BF16),
            jax.ShapeDtypeStruct((prefix, HEAD_DIM), BF16),
            jax.ShapeDtypeStruct((prefix, HEAD_DIM), BF16),
        ),
        in_specs=[any_space] * 3,
        out_specs=(any_space,) * 5,
        scratch_shapes=[
            pltpu.VMEM((rows, width), BF16),
            pltpu.VMEM((rows, two), BF16),
            pltpu.VMEM((prefix, two), BF16),
            dma((4,)),
            dma((6,)),
        ],
        compiler_params=pltpu.CompilerParams(vmem_limit_bytes=60 * 2**20),
        name="results",
    )(out, own, pre.reshape(prefix, two))


def solution(mesh):
    return jax.shard_map(
        shards,
        mesh=mesh,
        in_specs=(
            P("dp", "mp"),
            P("dp", "mp"),
            P("dp", "mp"),
            P("dp", "mp"),
            P("dp", "mp"),
            P("dp", "mp"),
            P(None, "mp"),
            P("dp"),
            P("dp", None),
        ),
        out_specs=(P("dp", "mp"), P("dp", "mp"), P("dp", "mp"), P("dp", "mp"), P("dp", "mp")),
        check_vma=False,
    )
```

```python
import functools

import jax
import jax.numpy as jnp
from jax import lax
from jax.experimental import pallas as pl
from jax.experimental.pallas import tpu as pltpu
from jax.sharding import PartitionSpec as P

HEAD_DIM = 128
PER_SOFTEN = 4
PER_GRADS = 4
GROUP = 16
SCALE = HEAD_DIM ** (-0.5)
LOG2E = 1.4426950408889634
MESH = pl.DeviceIdType.MESH
F32 = jnp.float32
BF16 = jnp.bfloat16


def dot(a, b):
    return jnp.dot(a, b, preferred_element_type=F32)


def dot_nt(a, b):
    return lax.dot_general(a, b, (((1,), (1,)), ((), ())), preferred_element_type=F32)


def fold(x, op):
    rows, cols = x.shape
    return op(x.reshape(rows // 8, 8, cols), axis=0)


def kernel(
    n,
    nmp,
    prompt_ref,
    lengths_ref,
    q_hbm,
    do_hbm,
    rk_hbm,
    rv_hbm,
    pk_hbm,
    pv_hbm,
    w_hbm,
    out_hbm,
    own_hbm,
    pre_hbm,
    q_v,
    do_v,
    own_v,
    w_v,
    table_v,
    stage_v,
    spread_v,
    choose_v,
    send_v,
    pre_v,
    keys_t,
    score_v,
    dprob_v,
    mask_v,
    inverse_v,
    grad_v,
    qg_v,
    ownout_v,
    back_v,
    gather_v,
    home_v,
    part_v,
    sib_v,
    hop_v,
    side_v,
    in_sem,
    w_sem,
    t_send,
    t_recv,
    s1_sem,
    s1_send,
    s1_recv,
    s2_send,
    s2_recv,
    b_send,
    b_recv,
    h_send,
    h_recv,
    sib_send,
    sib_recv,
    opp_send,
    opp_recv,
    raw_send,
    raw_recv,
    mix_send,
    mix_recv,
    out_sem,
):
    me = lax.axis_index("dp")
    mp = lax.axis_index("mp")
    ny = nmp // 2
    y, core = mp // 2, lax.rem(mp, 2)
    y_right, y_left, y_opp = lax.rem(y + 1, ny), lax.rem(y + ny - 1, ny), lax.rem(y + 2, ny)
    right, left, sibling = y_right * 2 + core, y_left * 2 + core, y * 2 + 1 - core
    blocks, block = q_v.shape[0], q_v.shape[1]
    chunk = send_v.shape[3]
    width = sib_v.shape[2]
    half = width // 2
    heads = q_v.shape[2] // HEAD_DIM
    tiles = score_v.shape[1] - 1
    per_tile = n // tiles

    def load(j, what, src, dst):
        return pltpu.make_async_copy(src, dst, in_sem.at[j, what])

    def own_loads(j):
        rows = pl.ds(j * block, block)
        return [
            load(j, 0, q_hbm.at[rows], q_v.at[j]),
            load(j, 1, do_hbm.at[rows], do_v.at[j]),
            load(j, 2, rk_hbm.at[rows], own_v.at[j, :, pl.ds(0, HEAD_DIM)]),
            load(j, 3, rv_hbm.at[rows], own_v.at[j, :, pl.ds(HEAD_DIM, HEAD_DIM)]),
        ]

    def w_load(dest):
        rows = pl.ds(pl.multiple_of(dest * width, width), width)
        return pltpu.make_async_copy(w_hbm.at[rows], w_v.at[rows], w_sem.at[dest])

    key_cols, value_cols = pl.ds(0, HEAD_DIM), pl.ds(HEAD_DIM, HEAD_DIM)
    side = n * GROUP

    def prompt_loads():
        return [
            pltpu.make_async_copy(src, stage_v.at[:, what], s1_sem.at[what])
            for what, src in enumerate((pk_hbm, pv_hbm))
        ]

    for copy in prompt_loads():
        copy.start()
    for j in range(blocks):
        for copy in own_loads(j):
            copy.start()

    side_x = 4 if n == 16 else n
    if n == 16:
        ones = [(0, 1), (0, 3), (1, 0), (3, 0), (1, 1), (3, 3), (1, 3), (3, 1)]
        offsets = ones + [(0, 2), (2, 0), (1, 2), (3, 2), (2, 1), (2, 3), (2, 2)]
    else:
        offsets = [(0, o) for o in range(1, n)]
    side_z = n // side_x
    my_z, my_x = me // side_x, lax.rem(me, side_x)
    peers = [
        lax.rem(my_z + dz, side_z) * side_x + lax.rem(my_x + dx, side_x) for dz, dx in offsets
    ]

    barrier = pltpu.get_barrier_semaphore()
    for peer in peers:
        pl.semaphore_signal(barrier, inc=1, device_id={"dp": peer}, device_id_type=MESH)
    for other in (right, left, sibling):
        pl.semaphore_signal(barrier, inc=1, device_id={"mp": other}, device_id_type=MESH)
    for j in range(blocks):
        table_v[me, j, :] = jnp.full((HEAD_DIM,), prompt_ref[j], jnp.int32)
    for copy in prompt_loads():
        copy.wait()
    pl.semaphore_wait(barrier, n - 1 + 3)

    def to_all(src, dst, send, recv):
        for peer in peers:
            pltpu.make_async_remote_copy(
                src_ref=src.at[peer],
                dst_ref=dst.at[me],
                send_sem=send,
                recv_sem=recv,
                device_id={"dp": peer},
                device_id_type=MESH,
            ).start()
        pltpu.make_async_copy(src.at[me], dst.at[me], recv).start()

    def load_weights():
        for dest in range(nmp):
            w_load(dest).start()

    def pick(j, what):
        for g in range(chunk // GROUP):
            rows = pl.ds(g * GROUP, GROUP)
            picked = dot(choose_v[j], spread_v[:, what, rows, :].reshape(side, HEAD_DIM))
            send_v[j, :, what, rows, :] = picked.astype(BF16).reshape(n, GROUP, HEAD_DIM)

    def hand_out(j, what=None):
        if what is None:
            to_all(send_v.at[j], pre_v.at[j], s2_send.at[j, 0], s2_recv.at[j, 0])
        else:
            sems = s2_send.at[j, what], s2_recv.at[j, what]
            to_all(send_v.at[j, :, what], pre_v.at[j, :, what], *sems)

    def arrived(ref, sem):
        pltpu.make_async_copy(ref, ref, sem).wait()

    def fetch():
        for peer in peers:
            pltpu.make_async_remote_copy(
                src_ref=table_v.at[me],
                dst_ref=table_v.at[me],
                send_sem=t_send,
                recv_sem=t_recv,
                device_id={"dp": peer},
                device_id_type=MESH,
            ).start()
        for what in range(2):
            to_all(stage_v.at[:, what], spread_v.at[:, what], s1_send.at[what], s1_recv.at[what])
        load_weights()
        row = lax.broadcasted_iota(jnp.int32, (side, side), 0)
        col = lax.broadcasted_iota(jnp.int32, (side, side), 1)
        same = lax.rem(row, GROUP) == lax.rem(col, GROUP)
        prompt_of_col = jnp.where(same, col // GROUP, -1)
        arrived(table_v.at[pl.ds(0, n - 1)], t_recv)

        for j in range(blocks):
            wanted = jnp.broadcast_to(table_v[:, j : j + 1, :], (n, GROUP, HEAD_DIM))
            wanted = wanted.reshape(side, HEAD_DIM)
            if side > HEAD_DIM:
                wanted = jnp.concatenate([wanted] * (side // HEAD_DIM), axis=1)
            else:
                wanted = wanted[:, :side]
            choose_v[j] = jnp.where(wanted == prompt_of_col, 1.0, 0.0).astype(BF16)

        for what in range(2):
            arrived(spread_v.at[:, what], s1_recv.at[what])
            pick(0, what)
            hand_out(0, what)
        for j in range(1, blocks):
            for what in range(2):
                pick(j, what)

    def part_of(j, t, what):
        if t == tiles:
            return own_v[j, :, (key_cols, value_cols)[what]]
        return pre_v[j, t * per_tile : (t + 1) * per_tile, what].reshape(block, HEAD_DIM)

    def visible(j):
        place = lax.broadcasted_iota(jnp.int32, (block, block), 1)
        key = lax.broadcasted_iota(jnp.int32, (block, block), 0)
        end = lengths_ref[j, 0]
        first = jnp.where(place >= end, end, 0)
        for s in range(1, lengths_ref.shape[1] - 1):
            end = end + lengths_ref[j, s]
            first = jnp.where(place >= end, end, first)
        return (key >= first) & (key <= place)

    def wait_keys(j):
        for copy in own_loads(j):
            copy.wait()
        arrived(pre_v.at[j, :, 0] if j == 0 else pre_v.at[j], s2_recv.at[j, 0])

    def wait_values(j):
        arrived(pre_v.at[j, :, 1], s2_recv.at[j, 1])

    def head_cols(h):
        return pl.ds(pl.multiple_of(h * HEAD_DIM, HEAD_DIM), HEAD_DIM)

    def soften(j):
        mask_v[...] = jnp.where(visible(j), 0.0, -1e30)
        for t in range(tiles + 1):
            keys_t[:, t * block : (t + 1) * block] = part_of(j, t, 0).T

        def scores(h):
            qh = q_v[j, :, head_cols(h)]
            top = None
            for t in range(tiles + 1):
                s = dot_nt(part_of(j, t, 0), qh)
                if t == tiles:
                    s = s + mask_v[...]
                score_v[h, t] = s
                got = fold(s, jnp.max)
                top = got if top is None else jnp.maximum(top, got)
            return jnp.max(top, axis=0, keepdims=True)

        def powers(h, top):
            total = jnp.zeros((8, block), F32)
            for t in range(tiles + 1):
                e = jnp.exp2((score_v[h, t] - top) * (SCALE * LOG2E))
                score_v[h, t] = e
                total += fold(e, jnp.sum)
            inverse = 1.0 / jnp.sum(total, axis=0, keepdims=True)
            inverse_v[h] = jnp.broadcast_to(inverse, (8, block))

        per = PER_SOFTEN

        def step(i, carry):
            hs = [i * per + s for s in range(per)]
            tops = [scores(h) for h in hs]
            for h, top in zip(hs, tops):
                powers(h, top)
            return carry

        lax.fori_loop(0, heads // per, step, 0)

    def attend(j, lower, upper):
        def middle(h, slot):
            doh = do_v[j, :, head_cols(h)]
            mixed = jnp.zeros((8, block), F32)
            for t in range(tiles + 1):
                dp = dot_nt(part_of(j, t, 1), doh)
                dprob_v[slot, t] = dp
                mixed += fold(score_v[h, t] * dp, jnp.sum)
            inverse = inverse_v[h, 0:1, :]
            return inverse, jnp.sum(mixed, axis=0, keepdims=True) * inverse

        def grads(hs, stats):
            qs = jnp.concatenate([q_v[j, :, head_cols(h)] for h in hs], axis=0)
            dos = jnp.concatenate([do_v[j, :, head_cols(h)] for h in hs], axis=0)
            dqs = [jnp.zeros((HEAD_DIM, block), F32) for _ in hs]
            for t in range(tiles + 1):
                dss, ps = [], []
                for slot, (inverse, delta) in enumerate(stats):
                    prob = score_v[hs[slot], t] * inverse
                    ds = (prob * (dprob_v[slot, t] - delta)).astype(BF16)
                    dss.append(ds)
                    ps.append(prob.astype(BF16))
                    dqs[slot] += dot(keys_t[:, t * block : (t + 1) * block], ds)
                grad_v[t, :, key_cols] += dot(jnp.concatenate(dss, axis=1), qs)
                grad_v[t, :, value_cols] += dot(jnp.concatenate(ps, axis=1), dos)
            for h, dq in zip(hs, dqs):
                qg_v[j, head_cols(h), :] = (dq * SCALE).astype(BF16)

        per = PER_GRADS

        def step(i, carry):
            hs = [i * per + s for s in range(per)]
            grads(hs, [middle(h, s) for s, h in enumerate(hs)])
            return carry

        if lower == 0:
            grad_v[...] = jnp.zeros_like(grad_v)
        lax.fori_loop(lower // per, upper // per, step, 0)

    def rounded(t):
        return jnp.concatenate(
            [grad_v[t, :, key_cols] * SCALE, grad_v[t, :, value_cols]], axis=1
        ).astype(BF16)

    def give_back(j):
        for t in range(tiles):
            back_v[j, t * per_tile : (t + 1) * per_tile] = rounded(t).reshape(
                per_tile, chunk, 2 * HEAD_DIM
            )
        ownout_v[j] = rounded(tiles)
        pltpu.make_async_copy(
            ownout_v.at[j], own_hbm.at[pl.ds(j * block, block)], out_sem.at[j, 0]
        ).start()

        to_all(back_v.at[j], gather_v.at[j], b_send.at[j], b_recv.at[j])

    def bring_home():
        for j in range(blocks):
            pltpu.make_async_copy(gather_v.at[j], gather_v.at[j], b_recv.at[j]).wait()
        chosen = [choose_v[j].astype(F32).T.astype(BF16) for j in range(blocks)]
        for g in range(chunk // GROUP):
            rows = pl.ds(g * GROUP, GROUP)
            added = jnp.zeros((side, 2 * HEAD_DIM), F32)
            for j in range(blocks):
                added += dot(chosen[j], gather_v[j, :, rows, :].reshape(side, 2 * HEAD_DIM))
            home_v[:, rows, :] = added.astype(BF16).reshape(n, GROUP, 2 * HEAD_DIM)

        to_all(home_v, pre_hbm, h_send, h_recv)

    def project(j, dest, first=0, last=2):
        if j == 0 and first == 0:
            w_load(dest).wait()
        step = width // 2

        def tile(i, carry):
            rows = pl.ds(pl.multiple_of(i * step, step), step)
            from_w = pl.ds(pl.multiple_of(dest * width + i * step, step), step)
            part_v[j, dest, rows, :] = dot(w_v[from_w, :], qg_v[j]).astype(BF16)
            return carry

        lax.fori_loop(first, last, tile, 0)

    def to_sibling(j, y_dest, slot):
        return pltpu.make_async_remote_copy(
            src_ref=part_v.at[j, y_dest * 2 + 1 - core],
            dst_ref=sib_v.at[j, slot],
            send_sem=sib_send.at[j, slot],
            recv_sem=sib_recv.at[j, slot],
            device_id={"mp": sibling},
            device_id_type=MESH,
        )

    def remote(src, dst, send, recv, dest):
        return pltpu.make_async_remote_copy(
            src_ref=src,
            dst_ref=dst,
            send_sem=send,
            recv_sem=recv,
            device_id={"mp": dest},
            device_id_type=MESH,
        )

    halves, ways = (pl.ds(0, half), pl.ds(half, half)), (right, left)
    pieces = 2
    piece = half // pieces

    def piece_rows(way, p):
        return pl.ds(way * half + p * piece, piece)

    def opposite(j, way, p):
        src = part_v.at[j, y_opp * 2 + core, piece_rows(way, p)]
        sems = opp_send.at[j, way, p], opp_recv.at[j, way, p]
        return remote(src, hop_v.at[j, way, pl.ds(p * piece, piece)], *sems, ways[way])

    def raw(j, way):
        rows = halves[1 - way]
        src, dst = part_v.at[j, ways[way], rows], side_v.at[j, way, rows]
        return remote(src, dst, raw_send.at[j, way], raw_recv.at[j, way], ways[way])

    def mixed(j, way, p):
        rows = piece_rows(way, p)
        src, dst = part_v.at[j, ways[way], rows], side_v.at[j, way, rows]
        return remote(src, dst, mix_send.at[j, way, p], mix_recv.at[j, way, p], ways[way])

    def add_sibling(j, y_dest, slot):
        mine = part_v[j, y_dest * 2 + core].astype(F32)
        part_v[j, y_dest * 2 + core] = (mine + sib_v[j, slot].astype(F32)).astype(BF16)

    def send_partials(j):
        project(j, y_opp * 2 + 1 - core)
        to_sibling(j, y_opp, 0).start()
        project(j, y_opp * 2 + core)
        project(j, y_right * 2 + 1 - core)
        to_sibling(j, y_right, 1).start()
        to_sibling(j, y_opp, 0).wait_recv()
        add_sibling(j, y_opp, 0)
        for p in range(pieces):
            for way in range(2):
                opposite(j, way, p).start()
        give_back(j)
        project(j, y_left * 2 + 1 - core)
        to_sibling(j, y_left, 2).start()
        project(j, y_right * 2 + core)
        project(j, y_left * 2 + core)
        to_sibling(j, y_right, 1).wait_recv()
        add_sibling(j, y_right, 1)
        raw(j, 0).start()
        project(j, y * 2 + 1 - core)
        to_sibling(j, y, 3).start()
        to_sibling(j, y_left, 2).wait_recv()
        add_sibling(j, y_left, 2)
        raw(j, 1).start()
        project(j, y * 2 + core)

    def pass_on(j, p):
        for way in range(2):
            opposite(j, way, p).wait_recv()
            rows = piece_rows(way, p)
            hop = hop_v[j, way, pl.ds(p * piece, piece), :].astype(F32)
            part_v[j, ways[way], rows, :] = (
                part_v[j, ways[way], rows, :].astype(F32) + hop
            ).astype(BF16)
            mixed(j, way, p).start()

    def out_copy(j, way, p):
        cols = piece_rows(way, p)
        rows = pl.ds(j * block, block)
        return pltpu.make_async_copy(
            q_v.at[j, :, cols], out_hbm.at[rows, cols], out_sem.at[j, 1 + way * pieces + p]
        )

    def finish(j):
        to_sibling(j, y, 3).wait_recv()
        for way in range(2):
            raw(j, way).wait_recv()
        for p in range(pieces):
            for way in range(2):
                rows = piece_rows(way, p)
                added = part_v[j, y * 2 + core, rows, :].astype(F32)
                added += sib_v[j, 3, rows, :].astype(F32)
                added += side_v[j, 1 - way, rows, :].astype(F32)
                mixed(j, way, p).wait_recv()
                added += side_v[j, way, rows, :].astype(F32)
                q_v[j, :, rows] = added.astype(BF16).T
                out_copy(j, way, p).start()

    def all_but_one(ref, sem):
        part = ref.at[pl.ds(0, n - 1)]
        pltpu.make_async_copy(part, part, sem).wait()

    def end_fetch():
        all_but_one(table_v, t_send)
        for what in range(2):
            all_but_one(spread_v.at[:, what], s1_send.at[what])
            all_but_one(send_v.at[0, :, what], s2_send.at[0, what])
        for j in range(1, blocks):
            all_but_one(send_v.at[j], s2_send.at[j, 0])

    def end_back():
        all_but_one(home_v, h_send)
        for j in range(blocks):
            all_but_one(back_v.at[j], b_send.at[j])
            pltpu.make_async_copy(
                ownout_v.at[j], own_hbm.at[pl.ds(j * block, block)], out_sem.at[j, 0]
            ).wait()
        pltpu.make_async_copy(pre_hbm, pre_hbm, h_recv).wait()

    def end_sum(j):
        for slot, y_dest in enumerate((y_opp, y_right, y_left, y)):
            to_sibling(j, y_dest, slot).wait_send()
        for way in range(2):
            raw(j, way).wait_send()
            for p in range(pieces):
                opposite(j, way, p).wait_send()
                mixed(j, way, p).wait_send()
                out_copy(j, way, p).wait()

    fetch()
    wait_keys(0)
    soften(0)
    wait_values(0)
    hand_out(1)
    attend(0, 0, heads)
    send_partials(0)
    wait_keys(1)
    soften(1)
    pass_on(0, 0)
    pass_on(0, 1)
    attend(1, 0, heads)
    send_partials(1)
    pass_on(1, 0)
    finish(0)
    pass_on(1, 1)
    bring_home()
    finish(1)
    end_fetch()
    end_back()
    for j in range(blocks):
        end_sum(j)


def results(out, own, pre, input_grad, key_grad, value_grad, pre_key_grad, pre_value_grad, *held):
    out_v, own_v, pre_v, load_sem, store_sem = held
    keys, values = pl.ds(0, HEAD_DIM), pl.ds(HEAD_DIM, HEAD_DIM)
    half = out.shape[0] // 2
    upper, lower = pl.ds(0, half), pl.ds(half, half)
    loads = [(out.at[r], out_v.at[r]) for r in (upper, lower)] + [(own, own_v), (pre, pre_v)]
    stores = [
        [(out_v.at[upper], input_grad.at[upper])],
        [(out_v.at[lower], input_grad.at[lower])],
        [(own_v.at[:, keys], key_grad), (own_v.at[:, values], value_grad)],
        [(pre_v.at[:, keys], pre_key_grad), (pre_v.at[:, values], pre_value_grad)],
    ]
    loads = [pltpu.make_async_copy(a, b, load_sem.at[i]) for i, (a, b) in enumerate(loads)]
    for copy in loads:
        copy.start()
    started = []
    for load, pairs in zip(loads, stores):
        load.wait()
        for a, b in pairs:
            copy = pltpu.make_async_copy(a, b, store_sem.at[len(started)])
            copy.start()
            started.append(copy)
    for copy in started:
        copy.wait()


def shards(
    queries,
    out_grad,
    response_keys,
    response_values,
    prefix_keys,
    prefix_values,
    q_weight,
    block_prompt,
    response_lengths,
):
    n, nmp = lax.axis_size("dp"), lax.axis_size("mp")
    blocks = block_prompt.shape[0]
    rows, cols = queries.shape
    block = rows // blocks
    prefix = prefix_keys.shape[0]
    chunk = prefix // n
    tiles = prefix // block
    width = q_weight.shape[0] // nmp
    two = 2 * HEAD_DIM
    dma = pltpu.SemaphoreType.DMA
    any_space = pl.BlockSpec(memory_space=pl.ANY)
    smem = pl.BlockSpec(memory_space=pltpu.SMEM)
    flops = 2 * rows * cols * (5 * (prefix + block) + q_weight.shape[0])
    out, own, pre = pl.pallas_call(
        functools.partial(kernel, n, nmp),
        out_shape=(
            jax.ShapeDtypeStruct((rows, width), BF16),
            jax.ShapeDtypeStruct((rows, two), BF16),
            jax.ShapeDtypeStruct((n, chunk, two), BF16),
        ),
        in_specs=[smem, smem] + [any_space] * 7,
        out_specs=(any_space,) * 3,
        scratch_shapes=[
            pltpu.VMEM((blocks, block, cols), BF16),
            pltpu.VMEM((blocks, block, cols), BF16),
            pltpu.VMEM((blocks, block, two), BF16),
            pltpu.VMEM(q_weight.shape, BF16),
            pltpu.VMEM((n, blocks, HEAD_DIM), jnp.int32),
            pltpu.VMEM((n, 2, chunk, HEAD_DIM), BF16),
            pltpu.VMEM((n, 2, chunk, HEAD_DIM), BF16),
            pltpu.VMEM((blocks, n * GROUP, n * GROUP), BF16),
            pltpu.VMEM((blocks, n, 2, chunk, HEAD_DIM), BF16),
            pltpu.VMEM((blocks, n, 2, chunk, HEAD_DIM), BF16),
            pltpu.VMEM((HEAD_DIM, prefix + block), BF16),
            pltpu.VMEM((cols // HEAD_DIM, tiles + 1, block, block), F32),
            pltpu.VMEM((PER_GRADS, tiles + 1, block, block), F32),
            pltpu.VMEM((block, block), F32),
            pltpu.VMEM((cols // HEAD_DIM, 8, block), F32),
            pltpu.VMEM((tiles + 1, block, two), F32),
            pltpu.VMEM((blocks, cols, block), BF16),
            pltpu.VMEM((blocks, block, two), BF16),
            pltpu.VMEM((blocks, n, chunk, two), BF16),
            pltpu.VMEM((blocks, n, chunk, two), BF16),
            pltpu.VMEM((n, chunk, two), BF16),
            pltpu.VMEM((blocks, nmp, width, block), BF16),
            pltpu.VMEM((blocks, nmp // 2, width, block), BF16),
            pltpu.VMEM((blocks, 2, width // 2, block), BF16),
            pltpu.VMEM((blocks, 2, width, block), BF16),
            dma((blocks, 4)),
            dma((nmp,)),
            dma,
            dma,
            dma((2,)),
            dma((2,)),
            dma((2,)),
            dma((blocks, 2)),
            dma((blocks, 2)),
            dma((blocks,)),
            dma((blocks,)),
            dma,
            dma,
            dma((blocks, 4)),
            dma((blocks, 4)),
            dma((blocks, 2, 2)),
            dma((blocks, 2, 2)),
            dma((blocks, 2)),
            dma((blocks, 2)),
            dma((blocks, 2, 2)),
            dma((blocks, 2, 2)),
            dma((blocks, 5)),
        ],
        compiler_params=pltpu.CompilerParams(
            collective_id=0, has_side_effects=True, vmem_limit_bytes=63 * 2**20
        ),
        cost_estimate=pl.CostEstimate(
            flops=flops, bytes_accessed=2 * q_weight.size, transcendentals=0
        ),
        name="attention_backward",
    )(
        block_prompt,
        response_lengths,
        queries,
        out_grad,
        response_keys,
        response_values,
        prefix_keys.reshape(n, chunk, HEAD_DIM),
        prefix_values.reshape(n, chunk, HEAD_DIM),
        q_weight,
    )
    return pl.pallas_call(
        results,
        out_shape=(
            jax.ShapeDtypeStruct((rows, width), BF16),
            jax.ShapeDtypeStruct((rows, HEAD_DIM), BF16),
            jax.ShapeDtypeStruct((rows, HEAD_DIM), BF16),
            jax.ShapeDtypeStruct((prefix, HEAD_DIM), BF16),
            jax.ShapeDtypeStruct((prefix, HEAD_DIM), BF16),
        ),
        in_specs=[any_space] * 3,
        out_specs=(any_space,) * 5,
        scratch_shapes=[
            pltpu.VMEM((rows, width), BF16),
            pltpu.VMEM((rows, two), BF16),
            pltpu.VMEM((prefix, two), BF16),
            dma((4,)),
            dma((6,)),
        ],
        compiler_params=pltpu.CompilerParams(vmem_limit_bytes=60 * 2**20),
        name="results",
    )(out, own, pre.reshape(prefix, two))


def solution(mesh):
    return jax.shard_map(
        shards,
        mesh=mesh,
        in_specs=(
            P("dp", "mp"),
            P("dp", "mp"),
            P("dp", "mp"),
            P("dp", "mp"),
            P("dp", "mp"),
            P("dp", "mp"),
            P(None, "mp"),
            P("dp"),
            P("dp", None),
        ),
        out_specs=(P("dp", "mp"), P("dp", "mp"), P("dp", "mp"), P("dp", "mp"), P("dp", "mp")),
        check_vma=False,
    )
```
